32 devices in a mesh: chan: 8 (over z, y), tm: 4 (over x, core).
Axes of the slice: x: 2, y: 2, z: 4, core: 2. Of those that a mesh axis runs over, the one named last changes fastest.
Arguments:
- strain_rate: float32 [2048, 4096], P('tm', 'chan'), may hold values from -6 to 6
- gauge: float32 [4096], P('chan'), may hold values from 0.02 to 0.2
- valid: int32 [4096], P('chan'), may hold values 0 or 1
- segment: int32 [4096], P('chan'), may hold values from 0 to 3, never falling along the last dimension, each value on 1 to 2048 neighbouring positions
- stencil: float32 [3, 4096], P(None, 'chan'), may hold values from 0.1 to 0.6
Outputs:
- strain_out: float32 [2048, 4096], P('tm', 'chan')
- velocity: float32 [2048, 4096], P('tm', 'chan')
The draws below stay inside these ranges and needn't reach their ends.
Inputs may be any that keep to these rules, and one draw needn't show every extreme that they name: Ids never fall along the fiber; each segment covers 1 to 2048 neighbouring channels, one exactly 2048.
All inputs are finite; a program needn't handle non-finite values. No bound on the sum of `valid` on one device may be relied on, other than what follows from the above.
Results may differ from the reference program's by a relative error of at most 0.0003.
Values sent between devices are 32-bit elements; how exact they have to be, the bound alone decides.
A program may use at most 64 MiB of HBM per device.

```python
import math
import jax
import jax.numpy as jnp
import numpy as np
from jax import lax

SL = 512
CH_DEV = 512
NT = 2048
CH = 4096
SEGMENTS = 4


def touch_ends(entries, stream_key, least, high):
    longest = entries.shape.index(max(entries.shape))
    spots = []
    for shift in (0, 1):
        where = [jax.random.randint(jax.random.fold_in(stream_key, axis), (), 0, length) for axis, length in enumerate(entries.shape)]
        where[longest] = (where[longest] + shift) % entries.shape[longest]
        spots.append(tuple(where))
    return entries.at[spots[0]].set(least).at[spots[1]].set(high)


def block_levels(stream_key, shape, shards, smallest, largest):
    def one(axis_at, parts):
        steps = jax.random.uniform(jax.random.fold_in(jax.random.fold_in(stream_key, 6), axis_at), (parts,), jnp.float32, smallest / len(shards), largest / len(shards))
        return jnp.repeat(jnp.exp(steps), shape[axis_at] // parts).reshape((-1,) + (1,) * (len(shape) - axis_at - 1))

    level = one(*shards[0])
    for cut in shards[1:]:
        level = level * one(*cut)
    return level


def length_profile(number_of, total, limit, lean):
    portions = [(1 << 20) // math.isqrt(standing ** lean) + 1 for standing in range(2, number_of + 1)]
    rest, counts = total - limit - (number_of - 1), [1] * (number_of - 1)
    while rest > 0:
        candidates = [i for i in range(number_of - 1) if counts[i] < limit]
        whole, remaining = sum([portions[i] for i in candidates]), rest
        for i in candidates:
            more = min(limit - counts[i], max(1, remaining * portions[i] // whole), rest)
            counts[i] = counts[i] + more
            rest = rest - more
    return np.array([limit] + counts)


def uneven(rng, number_of, total, limit, skew):
    if number_of == 2:
        one = jax.random.randint(rng, (), max(1, total - limit), min(limit, total - 1) + 1)
        return jnp.stack([one, total - one])
    tallies = jnp.asarray(length_profile(number_of, total, limit, skew), jnp.int32)
    couples = (number_of - 1) // 2
    donor, receiver = tallies[1:1 + 2 * couples:2], tallies[2:2 + 2 * couples:2]
    room = jnp.minimum(donor - 1, limit - receiver)
    moved = jax.random.randint(jax.random.fold_in(rng, 1), (couples,), 0, 1 << 20) % (room + 1)
    tallies = tallies.at[1:1 + 2 * couples:2].set(donor - moved).at[2:2 + 2 * couples:2].set(receiver + moved)
    return tallies[jax.random.permutation(jax.random.fold_in(rng, 2), number_of)]


def scatter_about(stream_key, extent, spread, reach, cuts=(), dtype=jnp.bfloat16):
    gain = block_levels(stream_key, extent, cuts, -0.22, 0.18) if cuts else 1.0
    values = jax.random.normal(stream_key, extent, jnp.float32) * spread * gain
    return jnp.minimum(jnp.maximum(values, -reach), reach).astype(dtype)


def setup_inputs(seed: int = 0) -> dict:
    keys = jax.random.split(jax.random.key(seed), 6)
    strain_rate = scatter_about(keys[0], (NT, CH), 1.0, 6.0, ((0, 4), (1, 8)), jnp.float32)
    gauge = jnp.clip(jnp.exp(math.log(0.2) - 2.3025851 * jax.random.uniform(keys[1], (CH,), jnp.float32) ** block_levels(keys[1], (CH,), ((0, 8),), -0.2, 0.2)), 0.02, 0.2)
    valid = touch_ends((jax.random.randint(keys[2], (CH,), 0, 8) < 7).astype(jnp.int32), jax.random.fold_in(keys[2], 1), 0, 1)
    segment = jnp.searchsorted(jnp.cumsum(uneven(keys[3], SEGMENTS, CH, 4 * CH_DEV, 1)), jnp.arange(CH), side="right").astype(jnp.int32)
    stencil = jnp.clip(0.1 + 0.5 * jax.random.uniform(keys[4], (3, CH), jnp.float32) ** block_levels(keys[4], (3, CH), ((1, 8),), -0.2, 0.2), 0.1, 0.6)
    return dict(strain_rate=strain_rate, gauge=gauge, valid=valid, segment=segment, stencil=stencil)


def reference(strain_rate, gauge, valid, segment, stencil):
    pole_one = 1.0 - 1.0 / (2.0 * SL)
    pole_two = 1.0 - 1.0 / (8.0 * SL)
    integ_gain = 1.0 / (8.0 * SL) ** 0.5
    zeros_row = jnp.zeros((CH,), jnp.float32)

    def advance(state, sample):
        lowone, lowtwo, strain = state
        lowone = pole_one * lowone + (1.0 - pole_one) * sample
        passone = sample - lowone
        lowtwo = pole_two * lowtwo + (1.0 - pole_two) * passone
        passtwo = passone - lowtwo
        strain = strain + integ_gain * passtwo
        return (lowone, lowtwo, strain), (passtwo, strain)

    final, (filtered, strain_out) = lax.scan(advance, (zeros_row, zeros_row, zeros_row), strain_rate)
    weight = gauge * valid.astype(jnp.float32)
    scaled = filtered * weight[None, :]

    def along(carry, column):
        running, previous = carry
        values, ident = column
        running = jnp.where(ident == previous, running + values, values)
        return (running, ident), running

    start = (jnp.zeros((NT,), jnp.float32), jnp.int32(-1))
    leftover, integrated = lax.scan(along, start, (scaled.T, segment))
    integrated = integrated.T
    padded = jnp.pad(integrated, ((0, 0), (1, 1)))
    velocity = stencil[0][None, :] * padded[:, :-2] + stencil[1][None, :] * padded[:, 1:-1] + stencil[2][None, :] * padded[:, 2:]
    return strain_out, velocity
```

```python
import functools

import jax
import jax.numpy as jnp
import ml_dtypes
import numpy as np
from jax import lax
from jax.experimental import pallas as pl
from jax.experimental.pallas import tpu as pltpu
from jax.sharding import PartitionSpec as P

LONGEST = 2048
F32 = jnp.float32
BF16 = jnp.bfloat16


def split_np(a):
    hi = a.astype(ml_dtypes.bfloat16)
    lo = (a - hi.astype(np.float64)).astype(ml_dtypes.bfloat16)
    return hi, lo


def time_constants(slab, part):
    p1 = 1.0 - 1.0 / (2.0 * slab)
    p2 = 1.0 - 1.0 / (8.0 * slab)
    gain = 1.0 / (8.0 * slab) ** 0.5
    k = np.arange(part, dtype=np.float64)
    off = k[:, None] - k[None, :]
    low = off >= 0
    safe = np.maximum(off, 0.0)
    g1 = np.where(low, (1.0 - p1) * p1**safe, 0.0)
    g2 = np.where(low, (1.0 - p2) * p2**safe, 0.0)
    one = np.eye(part)
    pass1 = one - g1
    low2 = g2 @ pass1
    filt = pass1 - low2
    integ = gain * np.cumsum(filt, axis=0)
    d1 = p1 ** (k + 1.0)
    d2 = p2 ** (k + 1.0)
    r1 = d1 - g2 @ d1
    c1 = gain * np.cumsum(r1)
    c2 = gain * np.cumsum(d2)
    rest = one - filt
    ends = np.stack([g1[-1], low2[-1], integ[-1]])
    trans = np.array(
        [[d1[-1], 0.0, 0.0], [r1[-1] - d1[-1], d2[-1], 0.0], [-c1[-1], -c2[-1], 1.0]]
    )
    strain_of = np.stack([-c1, -c2, np.ones(part)], axis=1)
    filt_of = np.stack([-r1, -d2, np.zeros(part)], axis=1)
    mats = np.stack([*split_np(integ), *split_np(rest)])
    e_hi, e_lo = split_np(ends)
    e_rows = np.zeros((16, part), ml_dtypes.bfloat16)
    e_rows[0:3], e_rows[3:6] = e_hi, e_lo
    cols = np.zeros((2, part, 16), ml_dtypes.bfloat16)
    for n, c in enumerate((strain_of, filt_of)):
        hi, lo = split_np(c)
        cols[n, :, 0:3], cols[n, :, 3:6], cols[n, :, 6:9] = hi, lo, hi
    return mats, e_rows, cols, trans


def split(a):
    hi = a.astype(BF16)
    return hi, (a - hi.astype(F32)).astype(BF16)


def mm(a, b):
    return jnp.dot(a, b, preferred_element_type=F32)


def kernel(
    n_chan, n_tm, reach, trans,
    x_hbm, gauge_hbm, valid_hbm, seg_hbm, sten_hbm, mats_hbm, ends_hbm, cols_hbm,
    strain_hbm, vel_hbm,
    x, gauge, valid, seg, sten, mats, ends, cols,
    xh, xl, vh, vl, u, strain, vel,
    right_out, left_out, right_in, left_in, state_out, state_in, st_rows,
    in_sem, out_sem, right_send, right_recv, left_send, left_recv, st_send, st_recv,
):
    slab, width = x.shape
    part = mats.shape[1]
    parts = slab // part
    tiles = width // 128
    ttiles = slab // 128
    j = lax.axis_index("chan")
    i = lax.axis_index("tm")

    blank = jnp.where(lax.broadcasted_iota(jnp.int32, (ttiles + 4, 128), 0) < ttiles, 0.0, -1.0)
    for d in range(reach):
        right_in[d] = blank
    left_in[...] = blank
    for d in range(n_tm - 1):
        state_in[d] = jnp.zeros((8, width), F32)

    barrier = pltpu.get_barrier_semaphore()
    for d in range(reach):
        @pl.when(j > d)
        def _():
            pl.semaphore_signal(barrier, inc=1, device_id={"chan": j - 1 - d, "tm": i})
    @pl.when(j < n_chan - 1)
    def _():
        pl.semaphore_signal(barrier, inc=1, device_id={"chan": j + 1, "tm": i})
    for d in range(n_tm - 1):
        @pl.when(i > d)
        def _():
            pl.semaphore_signal(barrier, inc=1, device_id={"chan": j, "tm": i - 1 - d})

    loads = [
        pltpu.make_async_copy(src, dst, in_sem.at[n])
        for n, (src, dst) in enumerate(
            [(gauge_hbm, gauge), (valid_hbm, valid), (seg_hbm, seg), (sten_hbm, sten),
             (x_hbm, x), (ends_hbm, ends), (cols_hbm, cols), (mats_hbm, mats)]
        )
    ]
    for c in loads:
        c.start()
    for c in loads[:4]:
        c.wait()

    ids = seg[...].astype(F32)
    w = gauge[...] * valid[...].astype(F32)
    lane = lax.broadcasted_iota(jnp.int32, (1, width), 1)
    tail = ids[:, width - 1:width]
    head = ids[:, 0:1]
    w_tail = jnp.where(ids == tail, w, 0.0)
    s0, s1 = sten[0:1, :], sten[1:2, :]
    s2_all = sten[2:3, :]
    s2 = jnp.where(lane == width - 1, 0.0, s2_all)
    edge = jnp.where(lane == width - 1, s2_all, 0.0)
    ids_prev = pltpu.roll(ids, 1, 1)
    ids_next = pltpu.roll(ids, width - 1, 1)

    def column(row):
        return jnp.transpose(jnp.broadcast_to(row, (128, 128)))

    def wide(block):
        return jnp.concatenate([block] * tiles, axis=1)

    for q in range(tiles):
        span = slice(q * 128, (q + 1) * 128)
        idc = wide(column(ids[:, span]))
        wc = wide(column(w[:, span]))
        gap = lax.broadcasted_iota(jnp.int32, (128, width), 1) - (
            lax.broadcasted_iota(jnp.int32, (128, width), 0) + q * 128
        )
        v = jnp.where((gap >= 1) & (idc == ids_prev), s0, 0.0)
        v = v + jnp.where((gap >= 0) & (idc == ids), s1, 0.0)
        v = v + jnp.where((gap >= -1) & (idc == ids_next), s2, 0.0)
        hi, lo = split(v * wc)
        vh[span, :] = hi
        vl[span, :] = lo

    loads[4].wait()
    eye = lax.broadcasted_iota(jnp.int32, (128, 128), 0) == lax.broadcasted_iota(
        jnp.int32, (128, 128), 1
    )
    w_first = w[:, 0:1]
    y = []
    for q in range(ttiles):
        span = slice(q * 128, (q + 1) * 128)
        block = x[span, :]
        yq = jnp.sum(block * w_tail, axis=1, keepdims=True)
        y.append(yq)
        right_out[q:q + 1, :] = jnp.sum(jnp.where(eye, yq, 0.0), axis=0, keepdims=True)
        left_out[q:q + 1, :] = jnp.sum(
            jnp.where(eye, block[:, 0:1] * w_first, 0.0), axis=0, keepdims=True
        )
    right_out[ttiles:, :] = jnp.broadcast_to(tail, (4, 128))
    left_out[ttiles:, :] = jnp.broadcast_to(head, (4, 128))

    targets = (
        jnp.minimum(reach, n_chan - 1 - j) + jnp.minimum(j, 1) + jnp.minimum(n_tm - 1, n_tm - 1 - i)
    )
    pl.semaphore_wait(barrier, targets)

    def to_right(d):
        return pltpu.make_async_remote_copy(
            right_out, right_in.at[d], right_send.at[d], right_recv.at[d],
            device_id={"chan": j + 1 + d, "tm": i},
        )

    def to_left():
        return pltpu.make_async_remote_copy(
            left_out, left_in, left_send, left_recv, device_id={"chan": j - 1, "tm": i}
        )

    def to_later(d):
        return pltpu.make_async_remote_copy(
            state_out, state_in.at[d], st_send.at[d], st_recv.at[d],
            device_id={"chan": j, "tm": i + 1 + d},
        )

    for d in range(reach):
        @pl.when(j + 1 + d < n_chan)
        def _():
            to_right(d).start()
    @pl.when(j > 0)
    def _():
        to_left().start()

    loads[5].wait()
    ends_x = []
    for k in range(parts):
        rows = slice(k * part, (k + 1) * part)
        hi, lo = split(x[rows, :])
        xh[rows, :] = hi
        xl[rows, :] = lo
        u[rows, :] = mm(hi, vh[...]) + mm(lo, vh[...]) + mm(hi, vl[...])
        e = mm(ends[...], hi) + mm(ends[...], lo)
        ends_x.append(e[0:3] + e[3:6])

    for d in range(reach):
        @pl.when(j > d)
        def _():
            to_right(d).wait_recv()
    @pl.when(j < n_chan - 1)
    def _():
        to_left().wait_recv()

    first = right_in[0]
    tail_prev = first[ttiles:ttiles + 1, :]
    carry = first[0:ttiles]
    for d in range(1, reach):
        far = right_in[d]
        carry = carry + jnp.where(far[ttiles:ttiles + 1, :] == tail_prev, far[0:ttiles], 0.0)
    beyond = left_in[...]
    tail_ids = jnp.concatenate([tail_prev] * tiles, axis=1)
    m = jnp.where(ids == tail_ids, 1.0, 0.0)
    m_prev = jnp.where(lane == 0, 1.0, pltpu.roll(m, 1, 1))
    m_next = pltpu.roll(m, width - 1, 1)
    a = s0 * m_prev + s1 * m + s2 * m_next
    m_tail = m[:, width - 1:width]
    same = jnp.where(beyond[ttiles:ttiles + 1, :] == tail, 1.0, 0.0)
    past = beyond[0:ttiles] + same * (right_out[0:ttiles, :] + m_tail * carry)
    for q in range(ttiles):
        span = slice(q * 128, (q + 1) * 128)
        cc = wide(column(carry[q:q + 1, :]))
        pc = column(past[q:q + 1, :])
        u[span, :] = u[span, :] + cc * a
        u[span, width - 128:] = u[span, width - 128:] + pc * edge[:, width - 128:]

    ends_u = []
    halves = []
    for k in range(parts):
        rows = slice(k * part, (k + 1) * part)
        hi, lo = split(u[rows, :])
        e = mm(ends[...], hi) + mm(ends[...], lo)
        ends_u.append(e[0:3] + e[3:6])
        halves.append((hi, lo))

    def combine(rows, coef):
        return [
            functools.reduce(
                lambda p, r: p + r,
                [float(coef[n, o]) * rows[o] for o in range(3) if coef[n, o] != 0.0],
            )
            for n in range(3)
        ]

    def rows_of(e):
        return [e[n:n + 1] for n in range(3)]

    def fold(list_of_ends):
        total = rows_of(list_of_ends[0])
        for e in list_of_ends[1:]:
            total = [p + r for p, r in zip(combine(total, trans), rows_of(e))]
        return total

    end_x, end_u = fold(ends_x), fold(ends_u)
    for n in range(3):
        state_out[n:n + 1, :] = end_x[n]
    for n in range(2):
        state_out[3 + n:4 + n, :] = end_u[n]
    state_out[5:8, :] = jnp.zeros((3, width), F32)

    for d in range(n_tm - 1):
        @pl.when(i + 1 + d < n_tm)
        def _():
            to_later(d).start()

    loads[6].wait()
    loads[7].wait()
    for k in range(parts):
        rows = slice(k * part, (k + 1) * part)
        strain[rows, :] = (
            mm(mats[0], xh[rows, :]) + mm(mats[0], xl[rows, :]) + mm(mats[1], xh[rows, :])
        )
        hi, lo = halves[k]
        vel[rows, :] = u[rows, :] - (mm(mats[2], hi) + mm(mats[2], lo) + mm(mats[3], hi))

    for d in range(n_tm - 1):
        @pl.when(i > d)
        def _():
            to_later(d).wait_recv()

    step = np.linalg.matrix_power(trans, parts)
    now_x = [jnp.zeros((1, width), F32)] * 3
    now_u = [jnp.zeros((1, width), F32)] * 3
    power = np.eye(3)
    for d in range(n_tm - 1):
        got = state_in[d]
        add_x = combine([got[n:n + 1] for n in range(3)], power)
        add_u = combine([got[3:4], got[4:5], jnp.zeros((1, width), F32)], power)
        now_x = [p + r for p, r in zip(now_x, add_x)]
        now_u = [p + r for p, r in zip(now_u, add_u)]
        power = step @ power

    st_rows[...] = jnp.zeros_like(st_rows)
    stores = []
    for k in range(parts):
        rows = slice(k * part, (k + 1) * part)
        for n, (now, dst, out) in enumerate(((now_x, strain, strain_hbm), (now_u, vel, vel_hbm))):
            slot = 2 * k + n
            for r in range(3):
                hi = now[r].astype(BF16).astype(F32)
                st_rows[slot, r:r + 1, :] = hi
                st_rows[slot, 3 + r:4 + r, :] = hi
                st_rows[slot, 6 + r:7 + r, :] = now[r] - hi
            dst[rows, :] = dst[rows, :] + mm(cols[n], st_rows[slot].astype(BF16))
            copy = pltpu.make_async_copy(dst.at[rows, :], out.at[rows, :], out_sem.at[slot])
            copy.start()
            stores.append(copy)
        if k + 1 < parts:
            now_x = [p + r for p, r in zip(combine(now_x, trans), rows_of(ends_x[k]))]
            now_u = [p + r for p, r in zip(combine(now_u, trans), rows_of(ends_u[k]))]

    for d in range(reach):
        @pl.when(j + 1 + d < n_chan)
        def _():
            to_right(d).wait_send()
    @pl.when(j > 0)
    def _():
        to_left().wait_send()
    for d in range(n_tm - 1):
        @pl.when(i + 1 + d < n_tm)
        def _():
            to_later(d).wait_send()
    for c in stores:
        c.wait()


def on_device(n_chan, n_tm, strain_rate, gauge, valid, segment, stencil):
    slab, width = strain_rate.shape
    part = 256 if slab % 256 == 0 else 128
    parts = slab // part
    reach = min(n_chan - 1, -(-LONGEST // width))
    mats, ends, cols, trans = time_constants(slab, part)
    ttiles = slab // 128
    any_spec = pl.BlockSpec(memory_space=pl.ANY)
    out = jax.ShapeDtypeStruct((slab, width), F32)
    return pl.pallas_call(
        functools.partial(kernel, n_chan, n_tm, reach, trans),
        out_shape=(out, out),
        in_specs=[any_spec] * 8,
        out_specs=(any_spec, any_spec),
        scratch_shapes=[
            pltpu.VMEM((slab, width), F32),
            pltpu.VMEM((1, width), F32),
            pltpu.VMEM((1, width), jnp.int32),
            pltpu.VMEM((1, width), jnp.int32),
            pltpu.VMEM((3, width), F32),
            pltpu.VMEM(mats.shape, BF16),
            pltpu.VMEM(ends.shape, BF16),
            pltpu.VMEM(cols.shape, BF16),
            pltpu.VMEM((slab, width), BF16),
            pltpu.VMEM((slab, width), BF16),
            pltpu.VMEM((width, width), BF16),
            pltpu.VMEM((width, width), BF16),
            pltpu.VMEM((slab, width), F32),
            pltpu.VMEM((slab, width), F32),
            pltpu.VMEM((slab, width), F32),
            pltpu.VMEM((ttiles + 4, 128), F32),
            pltpu.VMEM((ttiles + 4, 128), F32),
            pltpu.VMEM((reach, ttiles + 4, 128), F32),
            pltpu.VMEM((ttiles + 4, 128), F32),
            pltpu.VMEM((8, width), F32),
            pltpu.VMEM((n_tm - 1, 8, width), F32),
            pltpu.VMEM((2 * parts, 16, width), F32),
            pltpu.SemaphoreType.DMA((8,)),
            pltpu.SemaphoreType.DMA((2 * parts,)),
            pltpu.SemaphoreType.DMA((reach,)),
            pltpu.SemaphoreType.DMA((reach,)),
            pltpu.SemaphoreType.DMA,
            pltpu.SemaphoreType.DMA,
            pltpu.SemaphoreType.DMA((n_tm - 1,)),
            pltpu.SemaphoreType.DMA((n_tm - 1,)),
        ],
        compiler_params=pltpu.CompilerParams(
            collective_id=0, has_side_effects=True, vmem_limit_bytes=62 * 1024 * 1024
        ),
    )(
        strain_rate, gauge[None, :], valid[None, :], segment[None, :], stencil,
        jnp.asarray(mats), jnp.asarray(ends), jnp.asarray(cols),
    )


def solution(mesh):
    in_specs = (P("tm", "chan"), P("chan"), P("chan"), P("chan"), P(None, "chan"))
    out_specs = (P("tm", "chan"), P("tm", "chan"))
    return jax.shard_map(
        functools.partial(on_device, mesh.shape["chan"], mesh.shape["tm"]),
        mesh=mesh, in_specs=in_specs, out_specs=out_specs, check_vma=False,
    )
```

```python
import functools

import jax
import jax.numpy as jnp
import ml_dtypes
import numpy as np
from jax import lax
from jax.experimental import pallas as pl
from jax.experimental.pallas import tpu as pltpu
from jax.sharding import PartitionSpec as P

LONGEST = 2048
F32 = jnp.float32
BF16 = jnp.bfloat16


def split_np(a):
    hi = a.astype(ml_dtypes.bfloat16)
    lo = (a - hi.astype(np.float64)).astype(ml_dtypes.bfloat16)
    return hi, lo


def time_constants(slab, part):
    p1 = 1.0 - 1.0 / (2.0 * slab)
    p2 = 1.0 - 1.0 / (8.0 * slab)
    gain = 1.0 / (8.0 * slab) ** 0.5
    k = np.arange(part, dtype=np.float64)
    off = k[:, None] - k[None, :]
    low = off >= 0
    safe = np.maximum(off, 0.0)
    g1 = np.where(low, (1.0 - p1) * p1**safe, 0.0)
    g2 = np.where(low, (1.0 - p2) * p2**safe, 0.0)
    one = np.eye(part)
    pass1 = one - g1
    low2 = g2 @ pass1
    filt = pass1 - low2
    integ = gain * np.cumsum(filt, axis=0)
    d1 = p1 ** (k + 1.0)
    d2 = p2 ** (k + 1.0)
    r1 = d1 - g2 @ d1
    c1 = gain * np.cumsum(r1)
    c2 = gain * np.cumsum(d2)
    rest = one - filt
    ends = np.stack([g1[-1], low2[-1], integ[-1]])
    trans = np.array(
        [[d1[-1], 0.0, 0.0], [r1[-1] - d1[-1], d2[-1], 0.0], [-c1[-1], -c2[-1], 1.0]]
    )
    strain_of = np.stack([-c1, -c2, np.ones(part)], axis=1)
    filt_of = np.stack([-r1, -d2, np.zeros(part)], axis=1)
    mats = np.stack([*split_np(integ), *split_np(rest)])
    e_hi, e_lo = split_np(ends)
    e_rows = np.zeros((16, part), ml_dtypes.bfloat16)
    e_rows[0:3], e_rows[3:6] = e_hi, e_lo
    cols = np.zeros((2, part, 16), ml_dtypes.bfloat16)
    for n, c in enumerate((strain_of, filt_of)):
        hi, lo = split_np(c)
        cols[n, :, 0:3], cols[n, :, 3:6], cols[n, :, 6:9] = hi, lo, hi
    e_tiles = np.tile(ends.astype(np.float32).reshape(3, part // 128, 128), (1, slab // part, 1))
    return mats, e_rows, cols, trans, e_tiles


def split(a):
    hi = a.astype(BF16)
    return hi, (a - hi.astype(F32)).astype(BF16)


def mm(a, b):
    return jnp.dot(a, b, preferred_element_type=F32)


def kernel(
    n_chan, n_tm, reach, trans,
    x_hbm, gauge_hbm, valid_hbm, seg_hbm, sten_hbm, mats_hbm, ends_hbm, tiles_hbm,
    strain, vel, st_rows,
    x, gauge, valid, seg, sten, mats, ends, e_tiles,
    xh, xl, vh, vl, u,
    right_out, left_out, right_in, left_in, state_out, state_in,
    in_sem, right_send, right_recv, left_send, left_recv, st_send, st_recv,
):
    slab, width = x.shape
    part = mats.shape[1]
    parts = slab // part
    tiles = width // 128
    ttiles = slab // 128
    j = lax.axis_index("chan")
    i = lax.axis_index("tm")

    blank = jnp.where(lax.broadcasted_iota(jnp.int32, (ttiles + 4, 128), 0) < ttiles, 0.0, -1.0)
    for d in range(reach):
        right_in[d] = blank
    left_in[...] = blank
    for d in range(n_tm - 1):
        state_in[d] = jnp.zeros((8, width), F32)

    barrier = pltpu.get_barrier_semaphore()
    for d in range(reach):
        @pl.when(j > d)
        def _():
            pl.semaphore_signal(barrier, inc=1, device_id={"chan": j - 1 - d, "tm": i})
    @pl.when(j < n_chan - 1)
    def _():
        pl.semaphore_signal(barrier, inc=1, device_id={"chan": j + 1, "tm": i})
    for d in range(n_tm - 1):
        @pl.when(i > d)
        def _():
            pl.semaphore_signal(barrier, inc=1, device_id={"chan": j, "tm": i - 1 - d})

    loads = [
        pltpu.make_async_copy(src, dst, in_sem.at[n])
        for n, (src, dst) in enumerate(
            [(gauge_hbm, gauge), (valid_hbm, valid), (seg_hbm, seg), (sten_hbm, sten),
             (x_hbm, x), (ends_hbm, ends), (tiles_hbm, e_tiles), (mats_hbm, mats)]
        )
    ]
    for c in loads:
        c.start()
    for c in loads[:4]:
        c.wait()

    ids = seg[...].astype(F32)
    w = gauge[...] * valid[...].astype(F32)
    lane = lax.broadcasted_iota(jnp.int32, (1, width), 1)
    tail = ids[:, width - 1:width]
    head = ids[:, 0:1]
    w_tail = jnp.where(ids == tail, w, 0.0)
    s0, s1 = sten[0:1, :], sten[1:2, :]
    s2_all = sten[2:3, :]
    s2 = jnp.where(lane == width - 1, 0.0, s2_all)
    edge = jnp.where(lane == width - 1, s2_all, 0.0)
    ids_prev = pltpu.roll(ids, 1, 1)
    ids_next = pltpu.roll(ids, width - 1, 1)

    def column(row):
        return jnp.transpose(jnp.broadcast_to(row, (128, 128)))

    def wide(block):
        return jnp.concatenate([block] * tiles, axis=1)

    loads[4].wait()
    eye = lax.broadcasted_iota(jnp.int32, (128, 128), 0) == lax.broadcasted_iota(
        jnp.int32, (128, 128), 1
    )
    w_first = w[:, 0:1]
    y = []
    for q in range(ttiles):
        span = slice(q * 128, (q + 1) * 128)
        block = x[span, :]
        yq = jnp.sum(block * w_tail, axis=1, keepdims=True)
        y.append(yq)
        right_out[q:q + 1, :] = jnp.sum(jnp.where(eye, yq, 0.0), axis=0, keepdims=True)
        left_out[q:q + 1, :] = jnp.sum(
            jnp.where(eye, block[:, 0:1] * w_first, 0.0), axis=0, keepdims=True
        )
    right_out[ttiles:, :] = jnp.broadcast_to(tail, (4, 128))
    left_out[ttiles:, :] = jnp.broadcast_to(head, (4, 128))

    targets = (
        jnp.minimum(reach, n_chan - 1 - j) + jnp.minimum(j, 1) + jnp.minimum(n_tm - 1, n_tm - 1 - i)
    )
    pl.semaphore_wait(barrier, targets)

    def to_right(d):
        return pltpu.make_async_remote_copy(
            right_out, right_in.at[d], right_send.at[d], right_recv.at[d],
            device_id={"chan": j + 1 + d, "tm": i},
        )

    def to_left():
        return pltpu.make_async_remote_copy(
            left_out, left_in, left_send, left_recv, device_id={"chan": j - 1, "tm": i}
        )

    def to_later(d):
        return pltpu.make_async_remote_copy(
            state_out, state_in.at[d], st_send.at[d], st_recv.at[d],
            device_id={"chan": j, "tm": i + 1 + d},
        )

    for d in range(reach):
        @pl.when(j + 1 + d < n_chan)
        def _():
            to_right(d).start()
    @pl.when(j > 0)
    def _():
        to_left().start()

    for q in range(tiles):
        span = slice(q * 128, (q + 1) * 128)
        idc = wide(column(ids[:, span]))
        wc = wide(column(w[:, span]))
        gap = lax.broadcasted_iota(jnp.int32, (128, width), 1) - (
            lax.broadcasted_iota(jnp.int32, (128, width), 0) + q * 128
        )
        v = jnp.where((gap >= 1) & (idc == ids_prev), s0, 0.0)
        v = v + jnp.where((gap >= 0) & (idc == ids), s1, 0.0)
        v = v + jnp.where((gap >= -1) & (idc == ids_next), s2, 0.0)
        hi, lo = split(v * wc)
        vh[span, :] = hi
        vl[span, :] = lo

    loads[5].wait()
    ends_x, ends_u = [], []
    for k in range(parts):
        rows = slice(k * part, (k + 1) * part)
        hi, lo = split(x[rows, :])
        xh[rows, :] = hi
        xl[rows, :] = lo
        u[rows, :] = mm(hi, vh[...]) + mm(lo, vh[...]) + mm(hi, vl[...])
        e = mm(ends[...], hi) + mm(ends[...], lo)
        ends_x.append(e[0:3] + e[3:6])
        hi, lo = split(u[rows, :])
        e = mm(ends[...], hi) + mm(ends[...], lo)
        ends_u.append(e[0:3] + e[3:6])
    loads[6].wait()

    for d in range(reach):
        @pl.when(j > d)
        def _():
            to_right(d).wait_recv()
    @pl.when(j < n_chan - 1)
    def _():
        to_left().wait_recv()

    first = right_in[0]
    tail_prev = first[ttiles:ttiles + 1, :]
    carry = first[0:ttiles]
    for d in range(1, reach):
        far = right_in[d]
        carry = carry + jnp.where(far[ttiles:ttiles + 1, :] == tail_prev, far[0:ttiles], 0.0)
    beyond = left_in[...]
    tail_ids = jnp.concatenate([tail_prev] * tiles, axis=1)
    m = jnp.where(ids == tail_ids, 1.0, 0.0)
    m_prev = jnp.where(lane == 0, 1.0, pltpu.roll(m, 1, 1))
    m_next = pltpu.roll(m, width - 1, 1)
    a = s0 * m_prev + s1 * m + s2 * m_next
    m_tail = m[:, width - 1:width]
    same = jnp.where(beyond[ttiles:ttiles + 1, :] == tail, 1.0, 0.0)
    past = beyond[0:ttiles] + same * (right_out[0:ttiles, :] + m_tail * carry)
    per = part // 128
    for n in range(2):
        of_carry = jnp.sum(carry * e_tiles[n], axis=1, keepdims=True)
        of_past = jnp.sum(past * e_tiles[n], axis=1, keepdims=True)
        for k in range(parts):
            span = slice(k * per, (k + 1) * per)
            more = (
                jnp.sum(of_carry[span], axis=0, keepdims=True) * a
                + jnp.sum(of_past[span], axis=0, keepdims=True) * edge
            )
            ends_u[k] = ends_u[k] + jnp.where(
                lax.broadcasted_iota(jnp.int32, (3, width), 0) == n, more, 0.0
            )

    def combine(rows, coef):
        return [
            functools.reduce(
                lambda p, r: p + r,
                [float(coef[n, o]) * rows[o] for o in range(3) if coef[n, o] != 0.0],
            )
            for n in range(3)
        ]

    def rows_of(e):
        return [e[n:n + 1] for n in range(3)]

    def fold(list_of_ends):
        total = rows_of(list_of_ends[0])
        for e in list_of_ends[1:]:
            total = [p + r for p, r in zip(combine(total, trans), rows_of(e))]
        return total

    end_x, end_u = fold(ends_x), fold(ends_u)
    for n in range(3):
        state_out[n:n + 1, :] = end_x[n]
    for n in range(2):
        state_out[3 + n:4 + n, :] = end_u[n]
    state_out[5:8, :] = jnp.zeros((3, width), F32)

    for d in range(n_tm - 1):
        @pl.when(i + 1 + d < n_tm)
        def _():
            to_later(d).start()

    for q in range(ttiles):
        span = slice(q * 128, (q + 1) * 128)
        cc = wide(column(carry[q:q + 1, :]))
        pc = column(past[q:q + 1, :])
        u[span, :] = u[span, :] + cc * a
        u[span, width - 128:] = u[span, width - 128:] + pc * edge[:, width - 128:]

    loads[7].wait()
    for k in range(parts):
        rows = slice(k * part, (k + 1) * part)
        strain[rows, :] = (
            mm(mats[0], xh[rows, :]) + mm(mats[0], xl[rows, :]) + mm(mats[1], xh[rows, :])
        )
        hi, lo = split(u[rows, :])
        vel[rows, :] = u[rows, :] - (mm(mats[2], hi) + mm(mats[2], lo) + mm(mats[3], hi))

    for d in range(n_tm - 1):
        @pl.when(i > d)
        def _():
            to_later(d).wait_recv()

    step = np.linalg.matrix_power(trans, parts)
    now_x = [jnp.zeros((1, width), F32)] * 3
    now_u = [jnp.zeros((1, width), F32)] * 3
    power = np.eye(3)
    for d in range(n_tm - 1):
        got = state_in[d]
        add_x = combine([got[n:n + 1] for n in range(3)], power)
        add_u = combine([got[3:4], got[4:5], jnp.zeros((1, width), F32)], power)
        now_x = [p + r for p, r in zip(now_x, add_x)]
        now_u = [p + r for p, r in zip(now_u, add_u)]
        power = step @ power

    st_rows[...] = jnp.zeros_like(st_rows)
    for k in range(parts):
        for n, now in enumerate((now_x, now_u)):
            for r in range(3):
                hi = now[r].astype(BF16).astype(F32)
                st_rows[2 * k + n, r:r + 1, :] = hi
                st_rows[2 * k + n, 3 + r:4 + r, :] = hi
                st_rows[2 * k + n, 6 + r:7 + r, :] = now[r] - hi
        if k + 1 < parts:
            now_x = [p + r for p, r in zip(combine(now_x, trans), rows_of(ends_x[k]))]
            now_u = [p + r for p, r in zip(combine(now_u, trans), rows_of(ends_u[k]))]

    for d in range(reach):
        @pl.when(j + 1 + d < n_chan)
        def _():
            to_right(d).wait_send()
    @pl.when(j > 0)
    def _():
        to_left().wait_send()
    for d in range(n_tm - 1):
        @pl.when(i + 1 + d < n_tm)
        def _():
            to_later(d).wait_send()


def finish(strain, vel, st_rows, cols, strain_hbm, vel_hbm, buf, out_sem):
    slab = strain.shape[0]
    part = cols.shape[1]
    stores = []
    for k in range(slab // part):
        rows = slice(k * part, (k + 1) * part)
        for n, (src, out) in enumerate(((strain, strain_hbm), (vel, vel_hbm))):
            slot = 2 * k + n
            buf[slot] = src[rows, :] + mm(cols[n], st_rows[slot].astype(BF16))
            copy = pltpu.make_async_copy(buf.at[slot], out.at[rows, :], out_sem.at[slot])
            copy.start()
            stores.append(copy)
    for c in stores:
        c.wait()


def on_device(n_chan, n_tm, strain_rate, gauge, valid, segment, stencil):
    slab, width = strain_rate.shape
    part = 256 if slab % 256 == 0 else 128
    parts = slab // part
    reach = min(n_chan - 1, -(-LONGEST // width))
    mats, ends, cols, trans, e_tiles = time_constants(slab, part)
    ttiles = slab // 128
    hbm = pl.BlockSpec(memory_space=pltpu.HBM)
    any_spec = pl.BlockSpec(memory_space=pl.ANY)
    local = pl.BlockSpec(memory_space=pltpu.VMEM)
    out = jax.ShapeDtypeStruct((slab, width), F32)
    strain, vel, st_rows = pl.pallas_call(
        functools.partial(kernel, n_chan, n_tm, reach, trans),
        out_shape=(
            pltpu.VMEM((slab, width), F32),
            pltpu.VMEM((slab, width), F32),
            pltpu.VMEM((2 * parts, 16, width), F32),
        ),
        in_specs=[hbm] * 8,
        out_specs=(local, local, local),
        scratch_shapes=[
            pltpu.VMEM((slab, width), F32),
            pltpu.VMEM((1, width), F32),
            pltpu.VMEM((1, width), jnp.int32),
            pltpu.VMEM((1, width), jnp.int32),
            pltpu.VMEM((3, width), F32),
            pltpu.VMEM(mats.shape, BF16),
            pltpu.VMEM(ends.shape, BF16),
            pltpu.VMEM(e_tiles.shape, F32),
            pltpu.VMEM((slab, width), BF16),
            pltpu.VMEM((slab, width), BF16),
            pltpu.VMEM((width, width), BF16),
            pltpu.VMEM((width, width), BF16),
            pltpu.VMEM((slab, width), F32),
            pltpu.VMEM((ttiles + 4, 128), F32),
            pltpu.VMEM((ttiles + 4, 128), F32),
            pltpu.VMEM((reach, ttiles + 4, 128), F32),
            pltpu.VMEM((ttiles + 4, 128), F32),
            pltpu.VMEM((8, width), F32),
            pltpu.VMEM((n_tm - 1, 8, width), F32),
            pltpu.SemaphoreType.DMA((8,)),
            pltpu.SemaphoreType.DMA((reach,)),
            pltpu.SemaphoreType.DMA((reach,)),
            pltpu.SemaphoreType.DMA,
            pltpu.SemaphoreType.DMA,
            pltpu.SemaphoreType.DMA((n_tm - 1,)),
            pltpu.SemaphoreType.DMA((n_tm - 1,)),
        ],
        compiler_params=pltpu.CompilerParams(
            collective_id=0, has_side_effects=True, vmem_limit_bytes=32 * 1024 * 1024
        ),
    )(
        *[
            pltpu.with_memory_space_constraint(a, pltpu.HBM)
            for a in (
                strain_rate, gauge[None, :], valid[None, :], segment[None, :], stencil,
                jnp.asarray(mats), jnp.asarray(ends), jnp.asarray(e_tiles),
            )
        ],
    )
    return pl.pallas_call(
        finish,
        out_shape=(out, out),
        in_specs=[local] * 4,
        out_specs=(any_spec, any_spec),
        scratch_shapes=[
            pltpu.VMEM((2 * parts, part, width), F32),
            pltpu.SemaphoreType.DMA((2 * parts,)),
        ],
        compiler_params=pltpu.CompilerParams(vmem_limit_bytes=16 * 1024 * 1024),
    )(strain, vel, st_rows, jnp.asarray(cols))


def solution(mesh):
    in_specs = (P("tm", "chan"), P("chan"), P("chan"), P("chan"), P(None, "chan"))
    out_specs = (P("tm", "chan"), P("tm", "chan"))
    return jax.shard_map(
        functools.partial(on_device, mesh.shape["chan"], mesh.shape["tm"]),
        mesh=mesh, in_specs=in_specs, out_specs=out_specs, check_vma=False,
    )
```

```python
import functools

import jax
import jax.numpy as jnp
import ml_dtypes
import numpy as np
from jax import lax
from jax.experimental import pallas as pl
from jax.experimental.pallas import tpu as pltpu
from jax.sharding import PartitionSpec as P

LONGEST = 2048
F32 = jnp.float32
BF16 = jnp.bfloat16


def split_np(a):
    hi = a.astype(ml_dtypes.bfloat16)
    lo = (a - hi.astype(np.float64)).astype(ml_dtypes.bfloat16)
    return hi, lo


def time_constants(slab, part):
    p1 = 1.0 - 1.0 / (2.0 * slab)
    p2 = 1.0 - 1.0 / (8.0 * slab)
    gain = 1.0 / (8.0 * slab) ** 0.5
    k = np.arange(part, dtype=np.float64)
    off = k[:, None] - k[None, :]
    low = off >= 0
    safe = np.maximum(off, 0.0)
    g1 = np.where(low, (1.0 - p1) * p1**safe, 0.0)
    g2 = np.where(low, (1.0 - p2) * p2**safe, 0.0)
    one = np.eye(part)
    pass1 = one - g1
    low2 = g2 @ pass1
    filt = pass1 - low2
    integ = gain * np.cumsum(filt, axis=0)
    d1 = p1 ** (k + 1.0)
    d2 = p2 ** (k + 1.0)
    r1 = d1 - g2 @ d1
    c1 = gain * np.cumsum(r1)
    c2 = gain * np.cumsum(d2)
    rest = one - filt
    ends = np.stack([g1[-1], low2[-1], integ[-1]])
    trans = np.array(
        [[d1[-1], 0.0, 0.0], [r1[-1] - d1[-1], d2[-1], 0.0], [-c1[-1], -c2[-1], 1.0]]
    )
    strain_of = np.stack([-c1, -c2, np.ones(part)], axis=1)
    filt_of = np.stack([-r1, -d2, np.zeros(part)], axis=1)
    mats = np.stack([*split_np(integ), *split_np(rest)])
    e_hi, e_lo = split_np(ends)
    e_rows = np.zeros((16, part), ml_dtypes.bfloat16)
    e_rows[0:3], e_rows[3:6] = e_hi, e_lo
    cols = np.zeros((2, 16, part), np.float32)
    for n, c in enumerate((strain_of, filt_of)):
        hi, lo = split_np(c)
        cols[n, 0:3], cols[n, 3:6], cols[n, 6:9] = hi.T, lo.T, hi.T
    e_tiles = np.tile(ends.astype(np.float32).reshape(3, part // 128, 128), (1, slab // part, 1))
    return mats, e_rows, cols, trans, e_tiles


def split(a):
    hi = a.astype(BF16)
    return hi, (a - hi.astype(F32)).astype(BF16)


def mm_nt(a, b):
    return lax.dot_general(a, b, (((1,), (1,)), ((), ())), preferred_element_type=F32)


def mm_tn(a, b):
    return lax.dot_general(a, b, (((0,), (0,)), ((), ())), preferred_element_type=F32)


def mm(a, b):
    return jnp.dot(a, b, preferred_element_type=F32)


def kernel(
    n_chan, n_tm, reach, trans,
    x_hbm, gauge_hbm, valid_hbm, seg_hbm, sten_hbm, mats_hbm, ends_hbm, tiles_hbm, cols_hbm,
    strain, vel, st_rows, st_cols,
    x, gauge, valid, seg, sten, mats, ends, e_tiles, cols,
    xh, xl, vh, vl, pack,
    right_out, left_out, right_in, left_in, state_out, state_in,
    in_sem, right_send, right_recv, left_send, left_recv, st_send, st_recv,
):
    slab, width = x.shape
    part = mats.shape[1]
    parts = slab // part
    tiles = width // 128
    ttiles = slab // 128
    j = lax.axis_index("chan")
    i = lax.axis_index("tm")

    blank = jnp.where(lax.broadcasted_iota(jnp.int32, (ttiles + 4, 128), 0) < ttiles, 0.0, -1.0)
    for d in range(reach):
        right_in[d] = blank
    left_in[...] = blank
    for d in range(n_tm - 1):
        state_in[d] = jnp.zeros((8, width), F32)

    barrier = pltpu.get_barrier_semaphore()
    for d in range(reach):
        @pl.when(j > d)
        def _():
            pl.semaphore_signal(barrier, inc=1, device_id={"chan": j - 1 - d, "tm": i})
    @pl.when(j < n_chan - 1)
    def _():
        pl.semaphore_signal(barrier, inc=1, device_id={"chan": j + 1, "tm": i})
    for d in range(n_tm - 1):
        @pl.when(i > d)
        def _():
            pl.semaphore_signal(barrier, inc=1, device_id={"chan": j, "tm": i - 1 - d})

    loads = [
        pltpu.make_async_copy(src, dst, in_sem.at[n])
        for n, (src, dst) in enumerate(
            [(gauge_hbm, gauge), (valid_hbm, valid), (seg_hbm, seg), (sten_hbm, sten),
             (x_hbm, x), (ends_hbm, ends), (tiles_hbm, e_tiles), (cols_hbm, cols),
             (mats_hbm, mats)]
        )
    ]
    for c in loads[:8]:
        c.start()
    for c in loads[:4]:
        c.wait()

    ids = seg[...].astype(F32)
    w = gauge[...] * valid[...].astype(F32)
    lane = lax.broadcasted_iota(jnp.int32, (1, width), 1)
    tail = ids[:, width - 1:width]
    head = ids[:, 0:1]
    w_tail = jnp.where(ids == tail, w, 0.0)
    s0, s1 = sten[0:1, :], sten[1:2, :]
    s2_all = sten[2:3, :]
    s2 = jnp.where(lane == width - 1, 0.0, s2_all)
    edge = jnp.where(lane == width - 1, s2_all, 0.0)
    ids_prev = pltpu.roll(ids, 1, 1)
    ids_next = pltpu.roll(ids, width - 1, 1)

    def column(row):
        return jnp.transpose(jnp.broadcast_to(row, (128, 128)))

    def wide(block):
        return jnp.concatenate([block] * tiles, axis=1)

    for q in range(tiles):
        span = slice(q * 128, (q + 1) * 128)
        idc = wide(column(ids[:, span]))
        wc = wide(column(w[:, span]))
        gap = lax.broadcasted_iota(jnp.int32, (128, width), 1) - (
            lax.broadcasted_iota(jnp.int32, (128, width), 0) + q * 128
        )
        v = jnp.where((gap >= 1) & (idc == ids_prev), s0, 0.0)
        v = v + jnp.where((gap >= 0) & (idc == ids), s1, 0.0)
        v = v + jnp.where((gap >= -1) & (idc == ids_next), s2, 0.0)
        hi, lo = split(v * wc)
        vh[span, :] = hi
        vl[span, :] = lo

    loads[4].wait()
    loads[8].start()
    eye = lax.broadcasted_iota(jnp.int32, (128, 128), 0) == lax.broadcasted_iota(
        jnp.int32, (128, 128), 1
    )
    w_first = w[:, 0:1]
    y = []
    for q in range(ttiles):
        span = slice(q * 128, (q + 1) * 128)
        block = x[span, :]
        yq = jnp.sum(block * w_tail, axis=1, keepdims=True)
        y.append(yq)
        right_out[q:q + 1, :] = jnp.sum(jnp.where(eye, yq, 0.0), axis=0, keepdims=True)
        left_out[q:q + 1, :] = jnp.sum(
            jnp.where(eye, block[:, 0:1] * w_first, 0.0), axis=0, keepdims=True
        )
    right_out[ttiles:, :] = jnp.broadcast_to(tail, (4, 128))
    left_out[ttiles:, :] = jnp.broadcast_to(head, (4, 128))

    for k in range(parts):
        rows = slice(k * part, (k + 1) * part)
        hi, lo = split(x[rows, :])
        xh[rows, :] = hi
        xl[rows, :] = lo
    loads[8].wait()
    for k in range(parts):
        rows = slice(k * part, (k + 1) * part)
        strain[rows, :] = (
            mm(mats[0], xh[rows, :]) + mm(mats[0], xl[rows, :]) + mm(mats[1], xh[rows, :])
        )

    targets = (
        jnp.minimum(reach, n_chan - 1 - j) + jnp.minimum(j, 1) + jnp.minimum(n_tm - 1, n_tm - 1 - i)
    )
    pl.semaphore_wait(barrier, targets)

    def to_right(d):
        return pltpu.make_async_remote_copy(
            right_out, right_in.at[d], right_send.at[d], right_recv.at[d],
            device_id={"chan": j + 1 + d, "tm": i},
        )

    def to_left():
        return pltpu.make_async_remote_copy(
            left_out, left_in, left_send, left_recv, device_id={"chan": j - 1, "tm": i}
        )

    def to_later(d):
        return pltpu.make_async_remote_copy(
            state_out, state_in.at[d], st_send.at[d], st_recv.at[d],
            device_id={"chan": j, "tm": i + 1 + d},
        )

    for d in range(reach):
        @pl.when(j + 1 + d < n_chan)
        def _():
            to_right(d).start()
    @pl.when(j > 0)
    def _():
        to_left().start()

    for c in loads[5:8]:
        c.wait()
    ends_x, ends_u = [], []
    pack[...] = jnp.zeros_like(pack)
    for k in range(parts):
        rows = slice(k * part, (k + 1) * part)
        e = mm(ends[...], xh[rows, :]) + mm(ends[...], xl[rows, :])
        e = e[0:3] + e[3:6]
        ends_x.append(e)
        hi = e.astype(BF16).astype(F32)
        pack[k, 0:3, :] = hi
        pack[k, 8:11, :] = e - hi
    for k in range(parts):
        e = pack[k].astype(BF16)
        e = mm(e, vh[...]) + mm(e, vl[...])
        ends_u.append(e[0:3] + e[8:11])

    for d in range(reach):
        @pl.when(j > d)
        def _():
            to_right(d).wait_recv()
    @pl.when(j < n_chan - 1)
    def _():
        to_left().wait_recv()

    first = right_in[0]
    tail_prev = first[ttiles:ttiles + 1, :]
    carry = first[0:ttiles]
    for d in range(1, reach):
        far = right_in[d]
        carry = carry + jnp.where(far[ttiles:ttiles + 1, :] == tail_prev, far[0:ttiles], 0.0)
    beyond = left_in[...]
    tail_ids = jnp.concatenate([tail_prev] * tiles, axis=1)
    m = jnp.where(ids == tail_ids, 1.0, 0.0)
    m_prev = jnp.where(lane == 0, 1.0, pltpu.roll(m, 1, 1))
    m_next = pltpu.roll(m, width - 1, 1)
    a = s0 * m_prev + s1 * m + s2 * m_next
    m_tail = m[:, width - 1:width]
    same = jnp.where(beyond[ttiles:ttiles + 1, :] == tail, 1.0, 0.0)
    past = beyond[0:ttiles] + same * (right_out[0:ttiles, :] + m_tail * carry)
    per = part // 128
    for n in range(2):
        of_carry = jnp.sum(carry * e_tiles[n], axis=1, keepdims=True)
        of_past = jnp.sum(past * e_tiles[n], axis=1, keepdims=True)
        for k in range(parts):
            span = slice(k * per, (k + 1) * per)
            more = (
                jnp.sum(of_carry[span], axis=0, keepdims=True) * a
                + jnp.sum(of_past[span], axis=0, keepdims=True) * edge
            )
            ends_u[k] = ends_u[k] + jnp.where(
                lax.broadcasted_iota(jnp.int32, (3, width), 0) == n, more, 0.0
            )

    def combine(rows, coef):
        return [
            functools.reduce(
                lambda p, r: p + r,
                [float(coef[n, o]) * rows[o] for o in range(3) if coef[n, o] != 0.0],
            )
            for n in range(3)
        ]

    def rows_of(e):
        return [e[n:n + 1] for n in range(3)]

    def fold(list_of_ends):
        total = rows_of(list_of_ends[0])
        for e in list_of_ends[1:]:
            total = [p + r for p, r in zip(combine(total, trans), rows_of(e))]
        return total

    end_x, end_u = fold(ends_x), fold(ends_u)
    for n in range(3):
        state_out[n:n + 1, :] = end_x[n]
    for n in range(2):
        state_out[3 + n:4 + n, :] = end_u[n]
    state_out[5:8, :] = jnp.zeros((3, width), F32)

    for d in range(n_tm - 1):
        @pl.when(i + 1 + d < n_tm)
        def _():
            to_later(d).start()

    for k in range(parts):
        rows = slice(k * part, (k + 1) * part)
        u = mm(xh[rows, :], vh[...]) + mm(xl[rows, :], vh[...]) + mm(xh[rows, :], vl[...])
        hi, lo = split(u)
        vel[rows, :] = u - (mm(mats[2], hi) + mm(mats[2], lo) + mm(mats[3], hi))

    def flat(tile_rows, k):
        return jnp.concatenate([tile_rows[k * per + q:k * per + q + 1] for q in range(per)], axis=1)

    def put(ref, slot, row, value, order):
        hi = value.astype(BF16).astype(F32)
        lo = value - hi
        for n, which in enumerate(order):
            ref[slot, row + n:row + n + 1, :] = hi if which == "h" else lo

    st_rows[...] = jnp.zeros_like(st_rows)
    for k in range(parts):
        both = jnp.concatenate([flat(carry, k), flat(past, k)] + [jnp.zeros((6, part), F32)], axis=0)
        hi = both.astype(BF16).astype(F32)
        rows16 = jnp.concatenate([hi, both - hi], axis=0).astype(BF16)
        r = mm_nt(rows16, mats[2]) + mm_nt(rows16, mats[3])
        kept = both - (r[0:8] + r[8:16])
        st_cols[2 * k] = cols[0]
        st_cols[2 * k + 1] = cols[1]
        for n, coef in ((0, a), (1, edge)):
            put(st_cols, 2 * k + 1, 9 + 3 * n, kept[n:n + 1], "hlh")
            put(st_rows, 2 * k + 1, 9 + 3 * n, coef, "hhl")

    for d in range(n_tm - 1):
        @pl.when(i > d)
        def _():
            to_later(d).wait_recv()

    step = np.linalg.matrix_power(trans, parts)
    now_x = [jnp.zeros((1, width), F32)] * 3
    now_u = [jnp.zeros((1, width), F32)] * 3
    power = np.eye(3)
    for d in range(n_tm - 1):
        got = state_in[d]
        add_x = combine([got[n:n + 1] for n in range(3)], power)
        add_u = combine([got[3:4], got[4:5], jnp.zeros((1, width), F32)], power)
        now_x = [p + r for p, r in zip(now_x, add_x)]
        now_u = [p + r for p, r in zip(now_u, add_u)]
        power = step @ power

    for k in range(parts):
        for n, now in enumerate((now_x, now_u)):
            for r in range(3):
                hi = now[r].astype(BF16).astype(F32)
                st_rows[2 * k + n, r:r + 1, :] = hi
                st_rows[2 * k + n, 3 + r:4 + r, :] = hi
                st_rows[2 * k + n, 6 + r:7 + r, :] = now[r] - hi
        if k + 1 < parts:
            now_x = [p + r for p, r in zip(combine(now_x, trans), rows_of(ends_x[k]))]
            now_u = [p + r for p, r in zip(combine(now_u, trans), rows_of(ends_u[k]))]

    for d in range(reach):
        @pl.when(j + 1 + d < n_chan)
        def _():
            to_right(d).wait_send()
    @pl.when(j > 0)
    def _():
        to_left().wait_send()
    for d in range(n_tm - 1):
        @pl.when(i + 1 + d < n_tm)
        def _():
            to_later(d).wait_send()


def finish(strain, vel, st_rows, st_cols, strain_hbm, vel_hbm, buf, out_sem):
    slab = strain.shape[0]
    part = st_cols.shape[2]
    piece = buf.shape[1]
    stores = []
    for n, (src, out) in enumerate(((strain, strain_hbm), (vel, vel_hbm))):
        for p in range(slab // piece):
            k = p * piece // part
            rows = slice(p * piece, (p + 1) * piece)
            at = slice(p * piece - k * part, (p + 1) * piece - k * part)
            slot = n * (slab // piece) + p
            buf[slot] = src[rows, :] + mm_tn(
                st_cols[2 * k + n, :, at].astype(BF16), st_rows[2 * k + n].astype(BF16)
            )
            copy = pltpu.make_async_copy(buf.at[slot], out.at[rows, :], out_sem.at[slot])
            copy.start()
            stores.append(copy)
    for c in stores:
        c.wait()


def on_device(n_chan, n_tm, strain_rate, gauge, valid, segment, stencil):
    slab, width = strain_rate.shape
    part = 256 if slab % 256 == 0 else 128
    parts = slab // part
    reach = min(n_chan - 1, -(-LONGEST // width))
    mats, ends, cols, trans, e_tiles = time_constants(slab, part)
    ttiles = slab // 128
    hbm = pl.BlockSpec(memory_space=pltpu.HBM)
    any_spec = pl.BlockSpec(memory_space=pl.ANY)
    local = pl.BlockSpec(memory_space=pltpu.VMEM)
    out = jax.ShapeDtypeStruct((slab, width), F32)
    strain, vel, st_rows, st_cols = pl.pallas_call(
        functools.partial(kernel, n_chan, n_tm, reach, trans),
        out_shape=(
            pltpu.VMEM((slab, width), F32),
            pltpu.VMEM((slab, width), F32),
            pltpu.VMEM((2 * parts, 16, width), F32),
            pltpu.VMEM((2 * parts, 16, part), F32),
        ),
        in_specs=[hbm] * 9,
        out_specs=(local,) * 4,
        scratch_shapes=[
            pltpu.VMEM((slab, width), F32),
            pltpu.VMEM((1, width), F32),
            pltpu.VMEM((1, width), jnp.int32),
            pltpu.VMEM((1, width), jnp.int32),
            pltpu.VMEM((3, width), F32),
            pltpu.VMEM(mats.shape, BF16),
            pltpu.VMEM(ends.shape, BF16),
            pltpu.VMEM(e_tiles.shape, F32),
            pltpu.VMEM(cols.shape, F32),
            pltpu.VMEM((slab, width), BF16),
            pltpu.VMEM((slab, width), BF16),
            pltpu.VMEM((width, width), BF16),
            pltpu.VMEM((width, width), BF16),
            pltpu.VMEM((parts, 16, width), F32),
            pltpu.VMEM((ttiles + 4, 128), F32),
            pltpu.VMEM((ttiles + 4, 128), F32),
            pltpu.VMEM((reach, ttiles + 4, 128), F32),
            pltpu.VMEM((ttiles + 4, 128), F32),
            pltpu.VMEM((8, width), F32),
            pltpu.VMEM((n_tm - 1, 8, width), F32),
            pltpu.SemaphoreType.DMA((9,)),
            pltpu.SemaphoreType.DMA((reach,)),
            pltpu.SemaphoreType.DMA((reach,)),
            pltpu.SemaphoreType.DMA,
            pltpu.SemaphoreType.DMA,
            pltpu.SemaphoreType.DMA((n_tm - 1,)),
            pltpu.SemaphoreType.DMA((n_tm - 1,)),
        ],
        compiler_params=pltpu.CompilerParams(
            collective_id=0, has_side_effects=True, vmem_limit_bytes=32 * 1024 * 1024
        ),
    )(
        *[
            pltpu.with_memory_space_constraint(a, pltpu.HBM)
            for a in (
                strain_rate, gauge[None, :], valid[None, :], segment[None, :], stencil,
                jnp.asarray(mats), jnp.asarray(ends), jnp.asarray(e_tiles), jnp.asarray(cols),
            )
        ],
    )
    return pl.pallas_call(
        finish,
        out_shape=(out, out),
        in_specs=[local] * 4,
        out_specs=(any_spec, any_spec),
        scratch_shapes=[
            pltpu.VMEM((2 * ttiles, 128, width), F32),
            pltpu.SemaphoreType.DMA((2 * ttiles,)),
        ],
        compiler_params=pltpu.CompilerParams(vmem_limit_bytes=16 * 1024 * 1024),
    )(strain, vel, st_rows, st_cols)


def solution(mesh):
    in_specs = (P("tm", "chan"), P("chan"), P("chan"), P("chan"), P(None, "chan"))
    out_specs = (P("tm", "chan"), P("tm", "chan"))
    return jax.shard_map(
        functools.partial(on_device, mesh.shape["chan"], mesh.shape["tm"]),
        mesh=mesh, in_specs=in_specs, out_specs=out_specs, check_vma=False,
    )
```

```python
import functools

import jax
import jax.numpy as jnp
import ml_dtypes
import numpy as np
from jax import lax
from jax.experimental import pallas as pl
from jax.experimental.pallas import tpu as pltpu
from jax.sharding import PartitionSpec as P

LONGEST = 2048
F32 = jnp.float32
BF16 = jnp.bfloat16


def split_np(a):
    hi = a.astype(ml_dtypes.bfloat16)
    lo = (a - hi.astype(np.float64)).astype(ml_dtypes.bfloat16)
    return hi, lo


def time_constants(slab, part):
    p1 = 1.0 - 1.0 / (2.0 * slab)
    p2 = 1.0 - 1.0 / (8.0 * slab)
    gain = 1.0 / (8.0 * slab) ** 0.5
    k = np.arange(part, dtype=np.float64)
    off = k[:, None] - k[None, :]
    low = off >= 0
    safe = np.maximum(off, 0.0)
    g1 = np.where(low, (1.0 - p1) * p1**safe, 0.0)
    g2 = np.where(low, (1.0 - p2) * p2**safe, 0.0)
    one = np.eye(part)
    pass1 = one - g1
    low2 = g2 @ pass1
    filt = pass1 - low2
    integ = gain * np.cumsum(filt, axis=0)
    d1 = p1 ** (k + 1.0)
    d2 = p2 ** (k + 1.0)
    r1 = d1 - g2 @ d1
    c1 = gain * np.cumsum(r1)
    c2 = gain * np.cumsum(d2)
    rest = one - filt
    ends = np.stack([g1[-1], low2[-1], integ[-1]])
    trans = np.array(
        [[d1[-1], 0.0, 0.0], [r1[-1] - d1[-1], d2[-1], 0.0], [-c1[-1], -c2[-1], 1.0]]
    )
    strain_of = np.stack([-c1, -c2, np.ones(part)], axis=1)
    filt_of = np.stack([-r1, -d2, np.zeros(part)], axis=1)
    mats = np.stack([*split_np(integ), *split_np(rest)])
    e_hi, e_lo = split_np(ends)
    e_rows = np.zeros((16, part), ml_dtypes.bfloat16)
    e_rows[0:3], e_rows[3:6] = e_hi, e_lo
    cols = np.zeros((2, 16, part), np.float32)
    for n, c in enumerate((strain_of, filt_of)):
        hi, lo = split_np(c)
        cols[n, 0:3], cols[n, 3:6], cols[n, 6:9] = hi.T, lo.T, hi.T
    e_tiles = np.tile(ends.astype(np.float32).reshape(3, part // 128, 128), (1, slab // part, 1))
    return mats, e_rows, cols, trans, e_tiles


def split(a):
    hi = a.astype(BF16)
    return hi, (a - hi.astype(F32)).astype(BF16)


def mm_nt(a, b):
    return lax.dot_general(a, b, (((1,), (1,)), ((), ())), preferred_element_type=F32)


def mm_tn(a, b):
    return lax.dot_general(a, b, (((0,), (0,)), ((), ())), preferred_element_type=F32)


def mm(a, b):
    return jnp.dot(a, b, preferred_element_type=F32)


def kernel(
    n_chan, n_tm, reach, trans,
    x_hbm, gauge_hbm, valid_hbm, seg_hbm, sten_hbm, mats_hbm, ends_hbm, tiles_hbm, cols_hbm,
    strain, vel, st_rows, st_cols,
    x, gauge, valid, seg, sten, mats, ends, e_tiles, cols,
    xh, xl, vh, vl, pack,
    right_out, left_out, right_in, left_in, state_out, state_in,
    in_sem, right_send, right_recv, left_send, left_recv, st_send, st_recv,
):
    slab, width = x.shape
    part = mats.shape[1]
    parts = slab // part
    tiles = width // 128
    ttiles = slab // 128
    j = lax.axis_index("chan")
    i = lax.axis_index("tm")

    blank = jnp.where(lax.broadcasted_iota(jnp.int32, (ttiles + 4, 128), 0) < ttiles, 0.0, -1.0)
    for d in range(reach):
        right_in[d] = blank
    left_in[...] = blank
    for d in range(n_tm - 1):
        state_in[d] = jnp.zeros((8, width), F32)

    barrier = pltpu.get_barrier_semaphore()
    for d in range(reach):
        @pl.when(j > d)
        def _():
            pl.semaphore_signal(barrier, inc=1, device_id={"chan": j - 1 - d, "tm": i})
    @pl.when(j < n_chan - 1)
    def _():
        pl.semaphore_signal(barrier, inc=1, device_id={"chan": j + 1, "tm": i})
    for d in range(n_tm - 1):
        @pl.when(i > d)
        def _():
            pl.semaphore_signal(barrier, inc=1, device_id={"chan": j, "tm": i - 1 - d})

    loads = [
        pltpu.make_async_copy(src, dst, in_sem.at[n])
        for n, (src, dst) in enumerate(
            [(gauge_hbm, gauge), (valid_hbm, valid), (seg_hbm, seg), (sten_hbm, sten),
             (x_hbm, x), (ends_hbm, ends), (tiles_hbm, e_tiles), (cols_hbm, cols),
             (mats_hbm, mats)]
        )
    ]
    for c in loads[:8]:
        c.start()
    for c in loads[:4]:
        c.wait()

    ids = seg[...].astype(F32)
    w = gauge[...] * valid[...].astype(F32)
    lane = lax.broadcasted_iota(jnp.int32, (1, width), 1)
    tail = ids[:, width - 1:width]
    head = ids[:, 0:1]
    w_tail = jnp.where(ids == tail, w, 0.0)
    s0, s1 = sten[0:1, :], sten[1:2, :]
    s2_all = sten[2:3, :]
    s2 = jnp.where(lane == width - 1, 0.0, s2_all)
    edge = jnp.where(lane == width - 1, s2_all, 0.0)
    ids_prev = pltpu.roll(ids, 1, 1)
    ids_next = pltpu.roll(ids, width - 1, 1)

    def column(row):
        return jnp.transpose(jnp.broadcast_to(row, (128, 128)))

    def wide(block):
        return jnp.concatenate([block] * tiles, axis=1)

    for q in range(tiles):
        span = slice(q * 128, (q + 1) * 128)
        idc = wide(column(ids[:, span]))
        wc = wide(column(w[:, span]))
        gap = lax.broadcasted_iota(jnp.int32, (128, width), 1) - (
            lax.broadcasted_iota(jnp.int32, (128, width), 0) + q * 128
        )
        v = jnp.where((gap >= 1) & (idc == ids_prev), s0, 0.0)
        v = v + jnp.where((gap >= 0) & (idc == ids), s1, 0.0)
        v = v + jnp.where((gap >= -1) & (idc == ids_next), s2, 0.0)
        hi, lo = split(v * wc)
        vh[span, :] = hi
        vl[span, :] = lo

    loads[4].wait()
    loads[8].start()
    eye = lax.broadcasted_iota(jnp.int32, (128, 128), 0) == lax.broadcasted_iota(
        jnp.int32, (128, 128), 1
    )
    w_first = w[:, 0:1]
    y = []
    for q in range(ttiles):
        span = slice(q * 128, (q + 1) * 128)
        block = x[span, :]
        yq = jnp.sum(block * w_tail, axis=1, keepdims=True)
        y.append(yq)
        right_out[q:q + 1, :] = jnp.sum(jnp.where(eye, yq, 0.0), axis=0, keepdims=True)
        left_out[q:q + 1, :] = jnp.sum(
            jnp.where(eye, block[:, 0:1] * w_first, 0.0), axis=0, keepdims=True
        )
    right_out[ttiles:, :] = jnp.broadcast_to(tail, (4, 128))
    left_out[ttiles:, :] = jnp.broadcast_to(head, (4, 128))

    targets = (
        jnp.minimum(reach, n_chan - 1 - j) + jnp.minimum(j, 1) + jnp.minimum(n_tm - 1, n_tm - 1 - i)
    )
    pl.semaphore_wait(barrier, targets)

    def to_right(d):
        return pltpu.make_async_remote_copy(
            right_out, right_in.at[d], right_send.at[d], right_recv.at[d],
            device_id={"chan": j + 1 + d, "tm": i},
        )

    def to_left():
        return pltpu.make_async_remote_copy(
            left_out, left_in, left_send, left_recv, device_id={"chan": j - 1, "tm": i}
        )

    def to_later(d):
        return pltpu.make_async_remote_copy(
            state_out, state_in.at[d], st_send.at[d], st_recv.at[d],
            device_id={"chan": j, "tm": i + 1 + d},
        )

    for d in range(reach):
        @pl.when(j + 1 + d < n_chan)
        def _():
            to_right(d).start()
    @pl.when(j > 0)
    def _():
        to_left().start()

    for k in range(parts):
        rows = slice(k * part, (k + 1) * part)
        hi, lo = split(x[rows, :])
        xh[rows, :] = hi
        xl[rows, :] = lo
    for k in range(parts):
        rows = slice(k * part, (k + 1) * part)
        vel[rows, :] = mm(xh[rows, :], vh[...]) + mm(xl[rows, :], vh[...]) + mm(xh[rows, :], vl[...])
    for c in loads[5:8]:
        c.wait()
    ends_x, ends_u = [], []
    pack[...] = jnp.zeros_like(pack)
    for k in range(parts):
        rows = slice(k * part, (k + 1) * part)
        e = mm(ends[...], xh[rows, :]) + mm(ends[...], xl[rows, :])
        e = e[0:3] + e[3:6]
        ends_x.append(e)
        hi = e.astype(BF16).astype(F32)
        pack[k, 0:3, :] = hi
        pack[k, 8:11, :] = e - hi
    for k in range(parts):
        e = pack[k].astype(BF16)
        e = mm(e, vh[...]) + mm(e, vl[...])
        ends_u.append(e[0:3] + e[8:11])

    for d in range(reach):
        @pl.when(j > d)
        def _():
            to_right(d).wait_recv()
    @pl.when(j < n_chan - 1)
    def _():
        to_left().wait_recv()

    first = right_in[0]
    tail_prev = first[ttiles:ttiles + 1, :]
    carry = first[0:ttiles]
    for d in range(1, reach):
        far = right_in[d]
        carry = carry + jnp.where(far[ttiles:ttiles + 1, :] == tail_prev, far[0:ttiles], 0.0)
    beyond = left_in[...]
    tail_ids = jnp.concatenate([tail_prev] * tiles, axis=1)
    m = jnp.where(ids == tail_ids, 1.0, 0.0)
    m_prev = jnp.where(lane == 0, 1.0, pltpu.roll(m, 1, 1))
    m_next = pltpu.roll(m, width - 1, 1)
    a = s0 * m_prev + s1 * m + s2 * m_next
    m_tail = m[:, width - 1:width]
    same = jnp.where(beyond[ttiles:ttiles + 1, :] == tail, 1.0, 0.0)
    past = beyond[0:ttiles] + same * (right_out[0:ttiles, :] + m_tail * carry)
    per = part // 128
    for n in range(2):
        of_carry = jnp.sum(carry * e_tiles[n], axis=1, keepdims=True)
        of_past = jnp.sum(past * e_tiles[n], axis=1, keepdims=True)
        for k in range(parts):
            span = slice(k * per, (k + 1) * per)
            more = (
                jnp.sum(of_carry[span], axis=0, keepdims=True) * a
                + jnp.sum(of_past[span], axis=0, keepdims=True) * edge
            )
            ends_u[k] = ends_u[k] + jnp.where(
                lax.broadcasted_iota(jnp.int32, (3, width), 0) == n, more, 0.0
            )

    def combine(rows, coef):
        return [
            functools.reduce(
                lambda p, r: p + r,
                [float(coef[n, o]) * rows[o] for o in range(3) if coef[n, o] != 0.0],
            )
            for n in range(3)
        ]

    def rows_of(e):
        return [e[n:n + 1] for n in range(3)]

    def fold(list_of_ends):
        total = rows_of(list_of_ends[0])
        for e in list_of_ends[1:]:
            total = [p + r for p, r in zip(combine(total, trans), rows_of(e))]
        return total

    end_x, end_u = fold(ends_x), fold(ends_u)
    for n in range(3):
        state_out[n:n + 1, :] = end_x[n]
    for n in range(2):
        state_out[3 + n:4 + n, :] = end_u[n]
    state_out[5:8, :] = jnp.zeros((3, width), F32)

    for d in range(n_tm - 1):
        @pl.when(i + 1 + d < n_tm)
        def _():
            to_later(d).start()

    loads[8].wait()
    for k in range(parts):
        rows = slice(k * part, (k + 1) * part)
        strain[rows, :] = (
            mm(mats[0], xh[rows, :]) + mm(mats[0], xl[rows, :]) + mm(mats[1], xh[rows, :])
        )

    for k in range(parts):
        rows = slice(k * part, (k + 1) * part)
        u = vel[rows, :]
        hi, lo = split(u)
        vel[rows, :] = u - (mm(mats[2], hi) + mm(mats[2], lo) + mm(mats[3], hi))

    def flat(tile_rows, k):
        return jnp.concatenate([tile_rows[k * per + q:k * per + q + 1] for q in range(per)], axis=1)

    def put(ref, slot, row, value, order):
        hi = value.astype(BF16).astype(F32)
        lo = value - hi
        for n, which in enumerate(order):
            ref[slot, row + n:row + n + 1, :] = hi if which == "h" else lo

    st_rows[...] = jnp.zeros_like(st_rows)
    for k in range(parts):
        both = jnp.concatenate([flat(carry, k), flat(past, k)] + [jnp.zeros((6, part), F32)], axis=0)
        hi = both.astype(BF16).astype(F32)
        rows16 = jnp.concatenate([hi, both - hi], axis=0).astype(BF16)
        r = mm_nt(rows16, mats[2]) + mm_nt(rows16, mats[3])
        kept = both - (r[0:8] + r[8:16])
        st_cols[2 * k] = cols[0]
        st_cols[2 * k + 1] = cols[1]
        for n, coef in ((0, a), (1, edge)):
            put(st_cols, 2 * k + 1, 9 + 3 * n, kept[n:n + 1], "hlh")
            put(st_rows, 2 * k + 1, 9 + 3 * n, coef, "hhl")

    for d in range(n_tm - 1):
        @pl.when(i > d)
        def _():
            to_later(d).wait_recv()

    step = np.linalg.matrix_power(trans, parts)
    now_x = [jnp.zeros((1, width), F32)] * 3
    now_u = [jnp.zeros((1, width), F32)] * 3
    power = np.eye(3)
    for d in range(n_tm - 1):
        got = state_in[d]
        add_x = combine([got[n:n + 1] for n in range(3)], power)
        add_u = combine([got[3:4], got[4:5], jnp.zeros((1, width), F32)], power)
        now_x = [p + r for p, r in zip(now_x, add_x)]
        now_u = [p + r for p, r in zip(now_u, add_u)]
        power = step @ power

    for k in range(parts):
        for n, now in enumerate((now_x, now_u)):
            for r in range(3):
                hi = now[r].astype(BF16).astype(F32)
                st_rows[2 * k + n, r:r + 1, :] = hi
                st_rows[2 * k + n, 3 + r:4 + r, :] = hi
                st_rows[2 * k + n, 6 + r:7 + r, :] = now[r] - hi
        if k + 1 < parts:
            now_x = [p + r for p, r in zip(combine(now_x, trans), rows_of(ends_x[k]))]
            now_u = [p + r for p, r in zip(combine(now_u, trans), rows_of(ends_u[k]))]

    for d in range(reach):
        @pl.when(j + 1 + d < n_chan)
        def _():
            to_right(d).wait_send()
    @pl.when(j > 0)
    def _():
        to_left().wait_send()
    for d in range(n_tm - 1):
        @pl.when(i + 1 + d < n_tm)
        def _():
            to_later(d).wait_send()


def finish(strain, vel, st_rows, st_cols, strain_hbm, vel_hbm, buf, out_sem):
    slab = strain.shape[0]
    part = st_cols.shape[2]
    piece = buf.shape[1]
    stores = []
    for n, (src, out) in enumerate(((strain, strain_hbm), (vel, vel_hbm))):
        for p in range(slab // piece):
            k = p * piece // part
            rows = slice(p * piece, (p + 1) * piece)
            at = slice(p * piece - k * part, (p + 1) * piece - k * part)
            slot = n * (slab // piece) + p
            buf[slot] = src[rows, :] + mm_tn(
                st_cols[2 * k + n, :, at].astype(BF16), st_rows[2 * k + n].astype(BF16)
            )
            copy = pltpu.make_async_copy(buf.at[slot], out.at[rows, :], out_sem.at[slot])
            copy.start()
            stores.append(copy)
    for c in stores:
        c.wait()


def on_device(n_chan, n_tm, strain_rate, gauge, valid, segment, stencil):
    slab, width = strain_rate.shape
    part = 256 if slab % 256 == 0 else 128
    parts = slab // part
    reach = min(n_chan - 1, -(-LONGEST // width))
    mats, ends, cols, trans, e_tiles = time_constants(slab, part)
    ttiles = slab // 128
    hbm = pl.BlockSpec(memory_space=pltpu.HBM)
    any_spec = pl.BlockSpec(memory_space=pl.ANY)
    local = pl.BlockSpec(memory_space=pltpu.VMEM)
    out = jax.ShapeDtypeStruct((slab, width), F32)
    strain, vel, st_rows, st_cols = pl.pallas_call(
        functools.partial(kernel, n_chan, n_tm, reach, trans),
        out_shape=(
            pltpu.VMEM((slab, width), F32),
            pltpu.VMEM((slab, width), F32),
            pltpu.VMEM((2 * parts, 16, width), F32),
            pltpu.VMEM((2 * parts, 16, part), F32),
        ),
        in_specs=[hbm] * 9,
        out_specs=(local,) * 4,
        scratch_shapes=[
            pltpu.VMEM((slab, width), F32),
            pltpu.VMEM((1, width), F32),
            pltpu.VMEM((1, width), jnp.int32),
            pltpu.VMEM((1, width), jnp.int32),
            pltpu.VMEM((3, width), F32),
            pltpu.VMEM(mats.shape, BF16),
            pltpu.VMEM(ends.shape, BF16),
            pltpu.VMEM(e_tiles.shape, F32),
            pltpu.VMEM(cols.shape, F32),
            pltpu.VMEM((slab, width), BF16),
            pltpu.VMEM((slab, width), BF16),
            pltpu.VMEM((width, width), BF16),
            pltpu.VMEM((width, width), BF16),
            pltpu.VMEM((parts, 16, width), F32),
            pltpu.VMEM((ttiles + 4, 128), F32),
            pltpu.VMEM((ttiles + 4, 128), F32),
            pltpu.VMEM((reach, ttiles + 4, 128), F32),
            pltpu.VMEM((ttiles + 4, 128), F32),
            pltpu.VMEM((8, width), F32),
            pltpu.VMEM((n_tm - 1, 8, width), F32),
            pltpu.SemaphoreType.DMA((9,)),
            pltpu.SemaphoreType.DMA((reach,)),
            pltpu.SemaphoreType.DMA((reach,)),
            pltpu.SemaphoreType.DMA,
            pltpu.SemaphoreType.DMA,
            pltpu.SemaphoreType.DMA((n_tm - 1,)),
            pltpu.SemaphoreType.DMA((n_tm - 1,)),
        ],
        compiler_params=pltpu.CompilerParams(
            collective_id=0, has_side_effects=True, vmem_limit_bytes=32 * 1024 * 1024
        ),
    )(
        *[
            pltpu.with_memory_space_constraint(a, pltpu.HBM)
            for a in (
                strain_rate, gauge[None, :], valid[None, :], segment[None, :], stencil,
                jnp.asarray(mats), jnp.asarray(ends), jnp.asarray(e_tiles), jnp.asarray(cols),
            )
        ],
    )
    return pl.pallas_call(
        finish,
        out_shape=(out, out),
        in_specs=[local] * 4,
        out_specs=(any_spec, any_spec),
        scratch_shapes=[
            pltpu.VMEM((2 * ttiles, 128, width), F32),
            pltpu.SemaphoreType.DMA((2 * ttiles,)),
        ],
        compiler_params=pltpu.CompilerParams(vmem_limit_bytes=16 * 1024 * 1024),
    )(strain, vel, st_rows, st_cols)


def solution(mesh):
    in_specs = (P("tm", "chan"), P("chan"), P("chan"), P("chan"), P(None, "chan"))
    out_specs = (P("tm", "chan"), P("tm", "chan"))
    return jax.shard_map(
        functools.partial(on_device, mesh.shape["chan"], mesh.shape["tm"]),
        mesh=mesh, in_specs=in_specs, out_specs=out_specs, check_vma=False,
    )
```

```python
import functools

import jax
import jax.numpy as jnp
import ml_dtypes
import numpy as np
from jax import lax
from jax.experimental import pallas as pl
from jax.experimental.pallas import tpu as pltpu
from jax.sharding import PartitionSpec as P

LONGEST = 2048
F32 = jnp.float32
BF16 = jnp.bfloat16


def split_np(a):
    hi = a.astype(ml_dtypes.bfloat16)
    lo = (a - hi.astype(np.float64)).astype(ml_dtypes.bfloat16)
    return hi, lo


def time_constants(slab, part):
    p1 = 1.0 - 1.0 / (2.0 * slab)
    p2 = 1.0 - 1.0 / (8.0 * slab)
    gain = 1.0 / (8.0 * slab) ** 0.5
    k = np.arange(part, dtype=np.float64)
    off = k[:, None] - k[None, :]
    low = off >= 0
    safe = np.maximum(off, 0.0)
    g1 = np.where(low, (1.0 - p1) * p1**safe, 0.0)
    g2 = np.where(low, (1.0 - p2) * p2**safe, 0.0)
    one = np.eye(part)
    pass1 = one - g1
    low2 = g2 @ pass1
    filt = pass1 - low2
    integ = gain * np.cumsum(filt, axis=0)
    d1 = p1 ** (k + 1.0)
    d2 = p2 ** (k + 1.0)
    r1 = d1 - g2 @ d1
    c1 = gain * np.cumsum(r1)
    c2 = gain * np.cumsum(d2)
    rest = one - filt
    ends = np.stack([g1[-1], low2[-1], integ[-1]])
    trans = np.array(
        [[d1[-1], 0.0, 0.0], [r1[-1] - d1[-1], d2[-1], 0.0], [-c1[-1], -c2[-1], 1.0]]
    )
    strain_of = np.stack([-c1, -c2, np.ones(part)], axis=1)
    filt_of = np.stack([-r1, -d2, np.zeros(part)], axis=1)
    mats = np.stack([*split_np(integ), *split_np(rest)])
    e_hi, e_lo = split_np(ends)
    e_rows = np.zeros((16, part), ml_dtypes.bfloat16)
    e_rows[0:3], e_rows[3:6] = e_hi, e_lo
    cols = np.zeros((2, 16, part), np.float32)
    for n, c in enumerate((strain_of, filt_of)):
        hi, lo = split_np(c)
        cols[n, 0:3], cols[n, 3:6], cols[n, 6:9] = hi.T, lo.T, hi.T
    e_tiles = np.tile(ends.astype(np.float32).reshape(3, part // 128, 128), (1, slab // part, 1))
    return mats, e_rows, cols, trans, e_tiles


def split(a):
    hi = a.astype(BF16)
    return hi, (a - hi.astype(F32)).astype(BF16)


def mm_nt(a, b):
    return lax.dot_general(a, b, (((1,), (1,)), ((), ())), preferred_element_type=F32)


def mm_tn(a, b):
    return lax.dot_general(a, b, (((0,), (0,)), ((), ())), preferred_element_type=F32)


def mm(a, b):
    return jnp.dot(a, b, preferred_element_type=F32)


def kernel(
    n_chan, n_tm, reach, trans,
    x_hbm, gauge_hbm, valid_hbm, seg_hbm, sten_hbm, mats_hbm, ends_hbm, tiles_hbm, cols_hbm,
    strain, vel, st_rows, st_cols,
    x, gauge, valid, seg, sten, mats, ends, e_tiles, cols,
    xh, xl, vh, vl, pack,
    right_out, left_out, right_in, left_in, state_out, state_in,
    in_sem, right_send, right_recv, left_send, left_recv, st_send, st_recv,
):
    slab, width = x.shape
    part = mats.shape[1]
    parts = slab // part
    tiles = width // 128
    ttiles = slab // 128
    j = lax.axis_index("chan")
    i = lax.axis_index("tm")

    loads = [
        pltpu.make_async_copy(src, dst, in_sem.at[n])
        for n, (src, dst) in enumerate(
            [(gauge_hbm, gauge), (valid_hbm, valid), (seg_hbm, seg), (sten_hbm, sten),
             (x_hbm, x), (ends_hbm, ends), (tiles_hbm, e_tiles), (cols_hbm, cols),
             (mats_hbm, mats)]
        )
    ]
    for n in (4, 2, 0, 1, 3, 5, 6, 7):
        loads[n].start()

    blank = jnp.where(lax.broadcasted_iota(jnp.int32, (ttiles + 4, 128), 0) < ttiles, 0.0, -1.0)
    for d in range(reach):
        right_in[d] = blank
    left_in[...] = blank
    for d in range(n_tm - 1):
        state_in[d] = jnp.zeros((8, width), F32)

    barrier = pltpu.get_barrier_semaphore()
    for d in range(reach):
        @pl.when(j > d)
        def _():
            pl.semaphore_signal(barrier, inc=1, device_id={"chan": j - 1 - d, "tm": i})
    @pl.when(j < n_chan - 1)
    def _():
        pl.semaphore_signal(barrier, inc=1, device_id={"chan": j + 1, "tm": i})
    for d in range(n_tm - 1):
        @pl.when(i > d)
        def _():
            pl.semaphore_signal(barrier, inc=1, device_id={"chan": j, "tm": i - 1 - d})

    for c in loads[:4]:
        c.wait()

    ids = seg[...].astype(F32)
    w = gauge[...] * valid[...].astype(F32)
    lane = lax.broadcasted_iota(jnp.int32, (1, width), 1)
    tail = ids[:, width - 1:width]
    head = ids[:, 0:1]
    w_tail = jnp.where(ids == tail, w, 0.0)
    s0, s1 = sten[0:1, :], sten[1:2, :]
    s2_all = sten[2:3, :]
    s2 = jnp.where(lane == width - 1, 0.0, s2_all)
    edge = jnp.where(lane == width - 1, s2_all, 0.0)
    ids_prev = pltpu.roll(ids, 1, 1)
    ids_next = pltpu.roll(ids, width - 1, 1)

    def column(row):
        return jnp.transpose(jnp.broadcast_to(row, (128, 128)))

    def wide(block):
        return jnp.concatenate([block] * tiles, axis=1)

    for q in range(tiles):
        span = slice(q * 128, (q + 1) * 128)
        idc = wide(column(ids[:, span]))
        wc = wide(column(w[:, span]))
        gap = lax.broadcasted_iota(jnp.int32, (128, width), 1) - (
            lax.broadcasted_iota(jnp.int32, (128, width), 0) + q * 128
        )
        v = jnp.where((gap >= 1) & (idc == ids_prev), s0, 0.0)
        v = v + jnp.where((gap >= 0) & (idc == ids), s1, 0.0)
        v = v + jnp.where((gap >= -1) & (idc == ids_next), s2, 0.0)
        hi, lo = split(v * wc)
        vh[span, :] = hi
        vl[span, :] = lo

    loads[4].wait()
    loads[8].start()
    eye = lax.broadcasted_iota(jnp.int32, (128, 128), 0) == lax.broadcasted_iota(
        jnp.int32, (128, 128), 1
    )
    w_first = w[:, 0:1]
    y = []
    for q in range(ttiles):
        span = slice(q * 128, (q + 1) * 128)
        block = x[span, :]
        yq = jnp.sum(block * w_tail, axis=1, keepdims=True)
        y.append(yq)
        right_out[q:q + 1, :] = jnp.sum(jnp.where(eye, yq, 0.0), axis=0, keepdims=True)
        left_out[q:q + 1, :] = jnp.sum(
            jnp.where(eye, block[:, 0:1] * w_first, 0.0), axis=0, keepdims=True
        )
    right_out[ttiles:, :] = jnp.broadcast_to(tail, (4, 128))
    left_out[ttiles:, :] = jnp.broadcast_to(head, (4, 128))

    targets = (
        jnp.minimum(reach, n_chan - 1 - j) + jnp.minimum(j, 1) + jnp.minimum(n_tm - 1, n_tm - 1 - i)
    )
    pl.semaphore_wait(barrier, targets)

    def to_right(d):
        return pltpu.make_async_remote_copy(
            right_out, right_in.at[d], right_send.at[d], right_recv.at[d],
            device_id={"chan": j + 1 + d, "tm": i},
        )

    def to_left():
        return pltpu.make_async_remote_copy(
            left_out, left_in, left_send, left_recv, device_id={"chan": j - 1, "tm": i}
        )

    def to_later(d):
        return pltpu.make_async_remote_copy(
            state_out, state_in.at[d], st_send.at[d], st_recv.at[d],
            device_id={"chan": j, "tm": i + 1 + d},
        )

    for d in range(reach):
        @pl.when(j + 1 + d < n_chan)
        def _():
            to_right(d).start()
    @pl.when(j > 0)
    def _():
        to_left().start()

    for k in range(parts):
        rows = slice(k * part, (k + 1) * part)
        hi, lo = split(x[rows, :])
        xh[rows, :] = hi
        xl[rows, :] = lo
    for k in range(parts):
        rows = slice(k * part, (k + 1) * part)
        vel[rows, :] = mm(xh[rows, :], vh[...]) + mm(xl[rows, :], vh[...]) + mm(xh[rows, :], vl[...])
    for c in loads[5:8]:
        c.wait()
    ends_x, ends_u = [], []
    pack[...] = jnp.zeros_like(pack)
    for k in range(parts):
        rows = slice(k * part, (k + 1) * part)
        e = mm(ends[...], xh[rows, :]) + mm(ends[...], xl[rows, :])
        e = e[0:3] + e[3:6]
        ends_x.append(e)
        hi = e.astype(BF16).astype(F32)
        pack[k, 0:3, :] = hi
        pack[k, 8:11, :] = e - hi
    for k in range(parts):
        e = pack[k].astype(BF16)
        e = mm(e, vh[...]) + mm(e, vl[...])
        ends_u.append(e[0:3] + e[8:11])

    for d in range(reach):
        @pl.when(j > d)
        def _():
            to_right(d).wait_recv()
    @pl.when(j < n_chan - 1)
    def _():
        to_left().wait_recv()

    first = right_in[0]
    tail_prev = first[ttiles:ttiles + 1, :]
    carry = first[0:ttiles]
    for d in range(1, reach):
        far = right_in[d]
        carry = carry + jnp.where(far[ttiles:ttiles + 1, :] == tail_prev, far[0:ttiles], 0.0)
    beyond = left_in[...]
    tail_ids = jnp.concatenate([tail_prev] * tiles, axis=1)
    m = jnp.where(ids == tail_ids, 1.0, 0.0)
    m_prev = jnp.where(lane == 0, 1.0, pltpu.roll(m, 1, 1))
    m_next = pltpu.roll(m, width - 1, 1)
    a = s0 * m_prev + s1 * m + s2 * m_next
    m_tail = m[:, width - 1:width]
    same = jnp.where(beyond[ttiles:ttiles + 1, :] == tail, 1.0, 0.0)
    past = beyond[0:ttiles] + same * (right_out[0:ttiles, :] + m_tail * carry)
    per = part // 128
    for n in range(2):
        of_carry = jnp.sum(carry * e_tiles[n], axis=1, keepdims=True)
        of_past = jnp.sum(past * e_tiles[n], axis=1, keepdims=True)
        for k in range(parts):
            span = slice(k * per, (k + 1) * per)
            more = (
                jnp.sum(of_carry[span], axis=0, keepdims=True) * a
                + jnp.sum(of_past[span], axis=0, keepdims=True) * edge
            )
            ends_u[k] = ends_u[k] + jnp.where(
                lax.broadcasted_iota(jnp.int32, (3, width), 0) == n, more, 0.0
            )

    def combine(rows, coef):
        return [
            functools.reduce(
                lambda p, r: p + r,
                [float(coef[n, o]) * rows[o] for o in range(3) if coef[n, o] != 0.0],
            )
            for n in range(3)
        ]

    def rows_of(e):
        return [e[n:n + 1] for n in range(3)]

    def fold(list_of_ends):
        total = rows_of(list_of_ends[0])
        for e in list_of_ends[1:]:
            total = [p + r for p, r in zip(combine(total, trans), rows_of(e))]
        return total

    end_x, end_u = fold(ends_x), fold(ends_u)
    for n in range(3):
        state_out[n:n + 1, :] = end_x[n]
    for n in range(2):
        state_out[3 + n:4 + n, :] = end_u[n]
    state_out[5:8, :] = jnp.zeros((3, width), F32)

    for d in range(n_tm - 1):
        @pl.when(i + 1 + d < n_tm)
        def _():
            to_later(d).start()

    loads[8].wait()
    for k in range(parts):
        rows = slice(k * part, (k + 1) * part)
        strain[rows, :] = (
            mm(mats[0], xh[rows, :]) + mm(mats[0], xl[rows, :]) + mm(mats[1], xh[rows, :])
        )

    for k in range(parts):
        rows = slice(k * part, (k + 1) * part)
        u = vel[rows, :]
        hi, lo = split(u)
        vel[rows, :] = u - (mm(mats[2], hi) + mm(mats[2], lo) + mm(mats[3], hi))

    def flat(tile_rows, k):
        return jnp.concatenate([tile_rows[k * per + q:k * per + q + 1] for q in range(per)], axis=1)

    def put(ref, slot, row, value, order):
        hi = value.astype(BF16).astype(F32)
        lo = value - hi
        for n, which in enumerate(order):
            ref[slot, row + n:row + n + 1, :] = hi if which == "h" else lo

    st_rows[...] = jnp.zeros_like(st_rows)
    for k in range(parts):
        both = jnp.concatenate([flat(carry, k), flat(past, k)] + [jnp.zeros((6, part), F32)], axis=0)
        hi = both.astype(BF16).astype(F32)
        rows16 = jnp.concatenate([hi, both - hi], axis=0).astype(BF16)
        r = mm_nt(rows16, mats[2]) + mm_nt(rows16, mats[3])
        kept = both - (r[0:8] + r[8:16])
        st_cols[2 * k] = cols[0]
        st_cols[2 * k + 1] = cols[1]
        for n, coef in ((0, a), (1, edge)):
            put(st_cols, 2 * k + 1, 9 + 3 * n, kept[n:n + 1], "hlh")
            put(st_rows, 2 * k + 1, 9 + 3 * n, coef, "hhl")

    for d in range(n_tm - 1):
        @pl.when(i > d)
        def _():
            to_later(d).wait_recv()

    step = np.linalg.matrix_power(trans, parts)
    now_x = [jnp.zeros((1, width), F32)] * 3
    now_u = [jnp.zeros((1, width), F32)] * 3
    power = np.eye(3)
    for d in range(n_tm - 1):
        got = state_in[d]
        add_x = combine([got[n:n + 1] for n in range(3)], power)
        add_u = combine([got[3:4], got[4:5], jnp.zeros((1, width), F32)], power)
        now_x = [p + r for p, r in zip(now_x, add_x)]
        now_u = [p + r for p, r in zip(now_u, add_u)]
        power = step @ power

    for k in range(parts):
        for n, now in enumerate((now_x, now_u)):
            for r in range(3):
                hi = now[r].astype(BF16).astype(F32)
                st_rows[2 * k + n, r:r + 1, :] = hi
                st_rows[2 * k + n, 3 + r:4 + r, :] = hi
                st_rows[2 * k + n, 6 + r:7 + r, :] = now[r] - hi
        if k + 1 < parts:
            now_x = [p + r for p, r in zip(combine(now_x, trans), rows_of(ends_x[k]))]
            now_u = [p + r for p, r in zip(combine(now_u, trans), rows_of(ends_u[k]))]

    for d in range(reach):
        @pl.when(j + 1 + d < n_chan)
        def _():
            to_right(d).wait_send()
    @pl.when(j > 0)
    def _():
        to_left().wait_send()
    for d in range(n_tm - 1):
        @pl.when(i + 1 + d < n_tm)
        def _():
            to_later(d).wait_send()


def finish(strain, vel, st_rows, st_cols, strain_hbm, vel_hbm, buf, out_sem):
    slab = strain.shape[0]
    part = st_cols.shape[2]
    piece = buf.shape[1]
    stores = []
    for n, (src, out) in enumerate(((strain, strain_hbm), (vel, vel_hbm))):
        for p in range(slab // piece):
            k = p * piece // part
            rows = slice(p * piece, (p + 1) * piece)
            at = slice(p * piece - k * part, (p + 1) * piece - k * part)
            slot = n * (slab // piece) + p
            buf[slot] = src[rows, :] + mm_tn(
                st_cols[2 * k + n, :, at].astype(BF16), st_rows[2 * k + n].astype(BF16)
            )
            copy = pltpu.make_async_copy(buf.at[slot], out.at[rows, :], out_sem.at[slot])
            copy.start()
            stores.append(copy)
    for c in stores:
        c.wait()


def on_device(n_chan, n_tm, strain_rate, gauge, valid, segment, stencil):
    slab, width = strain_rate.shape
    part = 256 if slab % 256 == 0 else 128
    parts = slab // part
    reach = min(n_chan - 1, -(-LONGEST // width))
    mats, ends, cols, trans, e_tiles = time_constants(slab, part)
    ttiles = slab // 128
    hbm = pl.BlockSpec(memory_space=pltpu.HBM)
    any_spec = pl.BlockSpec(memory_space=pl.ANY)
    local = pl.BlockSpec(memory_space=pltpu.VMEM)
    out = jax.ShapeDtypeStruct((slab, width), F32)
    strain, vel, st_rows, st_cols = pl.pallas_call(
        functools.partial(kernel, n_chan, n_tm, reach, trans),
        out_shape=(
            pltpu.VMEM((slab, width), F32),
            pltpu.VMEM((slab, width), F32),
            pltpu.VMEM((2 * parts, 16, width), F32),
            pltpu.VMEM((2 * parts, 16, part), F32),
        ),
        in_specs=[hbm] * 9,
        out_specs=(local,) * 4,
        scratch_shapes=[
            pltpu.VMEM((slab, width), F32),
            pltpu.VMEM((1, width), F32),
            pltpu.VMEM((1, width), jnp.int32),
            pltpu.VMEM((1, width), jnp.int32),
            pltpu.VMEM((3, width), F32),
            pltpu.VMEM(mats.shape, BF16),
            pltpu.VMEM(ends.shape, BF16),
            pltpu.VMEM(e_tiles.shape, F32),
            pltpu.VMEM(cols.shape, F32),
            pltpu.VMEM((slab, width), BF16),
            pltpu.VMEM((slab, width), BF16),
            pltpu.VMEM((width, width), BF16),
            pltpu.VMEM((width, width), BF16),
            pltpu.VMEM((parts, 16, width), F32),
            pltpu.VMEM((ttiles + 4, 128), F32),
            pltpu.VMEM((ttiles + 4, 128), F32),
            pltpu.VMEM((reach, ttiles + 4, 128), F32),
            pltpu.VMEM((ttiles + 4, 128), F32),
            pltpu.VMEM((8, width), F32),
            pltpu.VMEM((n_tm - 1, 8, width), F32),
            pltpu.SemaphoreType.DMA((9,)),
            pltpu.SemaphoreType.DMA((reach,)),
            pltpu.SemaphoreType.DMA((reach,)),
            pltpu.SemaphoreType.DMA,
            pltpu.SemaphoreType.DMA,
            pltpu.SemaphoreType.DMA((n_tm - 1,)),
            pltpu.SemaphoreType.DMA((n_tm - 1,)),
        ],
        compiler_params=pltpu.CompilerParams(
            collective_id=0, has_side_effects=True, vmem_limit_bytes=32 * 1024 * 1024
        ),
    )(
        *[
            pltpu.with_memory_space_constraint(a, pltpu.HBM)
            for a in (
                strain_rate, gauge[None, :], valid[None, :], segment[None, :], stencil,
                jnp.asarray(mats), jnp.asarray(ends), jnp.asarray(e_tiles), jnp.asarray(cols),
            )
        ],
    )
    return pl.pallas_call(
        finish,
        out_shape=(out, out),
        in_specs=[local] * 4,
        out_specs=(any_spec, any_spec),
        scratch_shapes=[
            pltpu.VMEM((2 * ttiles, 128, width), F32),
            pltpu.SemaphoreType.DMA((2 * ttiles,)),
        ],
        compiler_params=pltpu.CompilerParams(vmem_limit_bytes=16 * 1024 * 1024),
    )(strain, vel, st_rows, st_cols)


def solution(mesh):
    in_specs = (P("tm", "chan"), P("chan"), P("chan"), P("chan"), P(None, "chan"))
    out_specs = (P("tm", "chan"), P("tm", "chan"))
    return jax.shard_map(
        functools.partial(on_device, mesh.shape["chan"], mesh.shape["tm"]),
        mesh=mesh, in_specs=in_specs, out_specs=out_specs, check_vma=False,
    )
```
